32 devices in a mesh: delay: 4 (over x, core), surface: 8 (over z, y).
Axes of the slice: x: 2, y: 2, z: 4, core: 2. Of those that a mesh axis runs over, the one named last changes fastest.
Arguments:
- lagged_block_entries: bfloat16 [4, 32, 16, 128, 128], P('delay', 'surface'), may hold values from -0.0625 to 0.0625
- pattern: int32 [4, 32, 16], P('delay', 'surface'), may hold values from 0 to 31, as said below
- diagonal_block_inverses: bfloat16 [32, 128, 128], P('surface'), may hold values from -0.5 to 0.5
- excitation: bfloat16 [6, 4096, 128], P(None, 'surface'), may hold values from -6 to 6
- history: float32 [4, 4096, 128], P('delay', 'surface'), may hold values from -6 to 6
Outputs:
- currents: bfloat16 [6, 4096, 128], P(None, 'surface')
- accum: float32 [4, 4096, 128], P('delay', 'surface')
The draws below stay inside these ranges and needn't reach their ends.
Inputs may be any that keep to these rules, and one draw needn't show every extreme that they name: `pattern`: in each row block i and lag, the 16 column block indices are distinct, and each names a block of the five groups of 4 blocks around i: block j lies in group floor(j / 4), and the groups g - 2 .. g + 2 around i's group g are counted cyclically over all 32 blocks.
All inputs are finite; a program needn't handle non-finite values.
Results may differ from the reference program's by a relative error of at most 0.0095.
Values may be sent and summed in bfloat16 or wider, within the bound.
No kernel may reach another device: no remote copies, remote signals or barrier semaphores. Data moves between devices by JAX's collectives and lax.ppermute only.
A program may use at most 64 MiB of HBM per device.

```python
import jax
import jax.numpy as jnp
from jax import lax

BS = 128
K = 16
R = 128
STEPS = 6
BLK_DEV = 4
LAGS = 4
NB = 32
N = 4096


def draw_pattern(key, part):
    window = 5 * BLK_DEV
    scores = jax.random.randint(key, (LAGS, NB, window), 0, 1 << 20) * window + jnp.arange(window, dtype=jnp.int32)
    _, selected_entries = lax.top_k(scores, K)
    owner = jnp.arange(NB, dtype=jnp.int32) // BLK_DEV
    base = (owner - 2) * BLK_DEV
    return ((base[None, :, None] + selected_entries.astype(jnp.int32)) % NB).astype(jnp.int32)


def block_scale(key, dims, shards, smallest, top_value):
    def one(dim, blocks):
        heights = jax.random.uniform(jax.random.fold_in(jax.random.fold_in(key, 6), dim), (blocks,), jnp.float32, smallest / len(shards), top_value / len(shards))
        return jnp.repeat(jnp.exp(heights), dims[dim] // blocks).reshape((-1,) + (1,) * (len(dims) - dim - 1))

    loudness = one(*shards[0])
    for cut in shards[1:]:
        loudness = loudness * one(*cut)
    return loudness


def centred(own_key, shape, spread, reach, cuts=(), kind=jnp.bfloat16):
    level = block_scale(own_key, shape, cuts, -0.22, 0.18) if cuts else 1.0
    array = jax.random.normal(own_key, shape, jnp.float32) * spread * level
    return jnp.minimum(jnp.maximum(array, -reach), reach).astype(kind)


def setup_inputs(seed: int = 0) -> dict:
    key_of = jax.random.split(jax.random.key(seed), 6)
    return {
        "lagged_block_entries": centred(key_of[0], (LAGS, NB, K, BS, BS), (4 * K * BS) ** -0.5, 0.0625, ((0, 4), (1, 8))),
        "pattern": draw_pattern(jax.random.fold_in(key_of[5], 71), 0),
        "diagonal_block_inverses": centred(key_of[2], (NB, BS, BS), BS ** -0.5, 0.5, ((0, 8),)),
        "excitation": centred(key_of[3], (STEPS, N, R), 1.0, 6.0, ((1, 8),)),
        "history": centred(key_of[4], (LAGS, N, R), 1.0, 6.0, ((0, 4), (1, 8)), jnp.float32),
    }


def reference(lagged_block_entries, pattern, diagonal_block_inverses, excitation, history):
    blocks_all = diagonal_block_inverses.shape[0]
    inverse_wide = diagonal_block_inverses.astype(jnp.float32)
    accum = history
    currents = []
    for step in range(STEPS):
        rhs = (excitation[step].astype(jnp.float32) - accum[0]).astype(jnp.bfloat16)
        fresh = jnp.einsum('ibc,icr->ibr', inverse_wide,
                           rhs.reshape(blocks_all, BS, R).astype(jnp.float32)).astype(jnp.bfloat16)

        def lag_product(pair):
            lag_offset, columns = pair
            selected_entries = fresh[columns].astype(jnp.float32)
            running_sum = jnp.einsum('dhxp,dhpl->dxl', lag_offset.astype(jnp.float32), selected_entries)
            return running_sum.reshape(blocks_all * BS, R)

        products = lax.map(lag_product, (lagged_block_entries, pattern))
        shifted = jnp.concatenate([accum[1:], jnp.zeros_like(accum[:1])], axis=0)
        accum = shifted + products
        currents.append(fresh.reshape(blocks_all * BS, R))
    return jnp.stack(currents), accum
```

```python
import functools

import jax
import jax.numpy as jnp
from jax import lax
from jax.experimental import pallas as pl
from jax.experimental.pallas import tpu as pltpu
from jax.sharding import PartitionSpec as P

F32 = jnp.float32
BF16 = jnp.bfloat16
AXES = ("delay", "surface")
VMEM = pl.BlockSpec(memory_space=pltpu.VMEM)
SMEM = pl.BlockSpec(memory_space=pltpu.SMEM)


def dot(a, b):
    return jnp.dot(a, b, preferred_element_type=F32)


def call(body, outs, flops, args):
    moved = sum(a.size * a.dtype.itemsize for a in args)
    return pl.pallas_call(
        body,
        out_shape=outs,
        in_specs=[SMEM] + [VMEM] * (len(args) - 1),
        out_specs=tuple(VMEM for _ in outs),
        cost_estimate=pl.CostEstimate(flops=flops, bytes_accessed=moved, transcendentals=0),
        compiler_params=pltpu.CompilerParams(vmem_limit_bytes=24 * 1024 * 1024),
    )(*args)


def spread_body(slots, slot_ref, entries_ref, keep_ref, send_ref):
    row = pl.program_id(0)
    size = entries_ref.shape[-1]
    count = keep_ref.shape[1] // size
    for out_ref, first in ((keep_ref, 0), (send_ref, count)):
        for j in range(count):
            slot = slot_ref[row, first + j]
            columns = slice(j * size, (j + 1) * size)

            @pl.when(slot < slots)
            def _():
                out_ref[:, columns] = entries_ref[0, jnp.minimum(slot, slots - 1)]

            @pl.when(slot >= slots)
            def _():
                out_ref[:, columns] = jnp.zeros((out_ref.shape[0], size), out_ref.dtype)


def spread(entries, slot):
    blocks, slots, size, _ = entries.shape
    width = slot.shape[1] // 2 * size
    out = jax.ShapeDtypeStruct((blocks * size, width), entries.dtype)
    return pl.pallas_call(
        functools.partial(spread_body, slots),
        grid_spec=pltpu.PrefetchScalarGridSpec(
            num_scalar_prefetch=1,
            grid=(blocks,),
            in_specs=[pl.BlockSpec((1, slots, size, size), lambda i, s: (i, 0, 0, 0))],
            out_specs=[pl.BlockSpec((size, width), lambda i, s: (i, 0))] * 2,
        ),
        out_shape=(out, out),
        compiler_params=pltpu.CompilerParams(vmem_limit_bytes=24 * 1024 * 1024),
    )(slot, entries)


def own_half(flags, current_ref):
    rows = current_ref.shape[0] // 2
    return current_ref[pl.ds(pl.multiple_of(flags[0] * rows, rows), rows), :]


def early_body(flags, near_ref, far_ref, now_ref, first_ref, second_ref, before_ref, out_ref):
    rows = now_ref.shape[0]
    out_ref[...] = (
        dot(near_ref[:, 2 * rows :], own_half(flags, now_ref))
        + dot(far_ref[:, :rows], first_ref[...])
        + dot(far_ref[:, rows : 2 * rows], second_ref[...])
        + dot(far_ref[:, 2 * rows :], own_half(flags, before_ref))
    )


def early_first_body(flags, near_ref, now_ref, out_ref):
    rows = now_ref.shape[0]
    out_ref[...] = dot(near_ref[:, 2 * rows :], own_half(flags, now_ref))


def late_body(flags, near_ref, first_ref, second_ref, early_ref, out_ref):
    rows = first_ref.shape[0]
    out_ref[...] = (
        early_ref[...]
        + dot(near_ref[:, :rows], first_ref[...])
        + dot(near_ref[:, rows : 2 * rows], second_ref[...])
    )


def late_final_body(
    flags, near_ref, far_ref, now_ref, first_ref, second_ref, early_ref, keep_ref, send_ref
):
    rows = first_ref.shape[0]
    even = (
        early_ref[...]
        + dot(near_ref[:, :rows], first_ref[...])
        + dot(near_ref[:, rows : 2 * rows], second_ref[...])
    )
    odd = (
        dot(far_ref[:, :rows], first_ref[...])
        + dot(far_ref[:, rows : 2 * rows], second_ref[...])
        + dot(far_ref[:, 2 * rows :], own_half(flags, now_ref))
    )
    ends = flags[2] == 1
    second_core = flags[0] == 1
    keep_ref[...] = jnp.where(ends & second_core, odd, even)
    send_ref[...] = jnp.where(ends & ~second_core, odd, even)


def solve(inverse_ref, rhs, out_ref, keep, other):
    size = inverse_ref.shape[1]
    for i in range(inverse_ref.shape[0]):
        rows = slice(i * size, (i + 1) * size)
        fresh = dot(inverse_ref[i], rhs[rows]).astype(BF16)
        out_ref[rows, :] = jnp.where(keep, fresh, other[rows])


def start_body(flags, inverse_ref, excitation_ref, history_ref, out_ref):
    rhs = (excitation_ref[...].astype(F32) - history_ref[...]).astype(BF16)
    solve(inverse_ref, rhs, out_ref, flags[1] == 0, jnp.zeros_like(rhs))


def next_body(
    special, flags, inverse_ref, excitation_ref, mine_ref, other_ref, field_in_ref,
    current_in_ref, *rest
):
    *history, out_ref, field_ref = rest
    came = jnp.where(flags[3] == 1, 0.0, field_in_ref[...].astype(F32))
    if special:
        came = jnp.where(flags[4] == 1, history[0][...], came)
    field = mine_ref[...] + other_ref[...] + came
    rhs = (excitation_ref[...].astype(F32) - field).astype(BF16)
    first_pair = flags[1] == 0
    solve(inverse_ref, rhs, out_ref, first_pair, current_in_ref)
    field_ref[...] = field.astype(BF16)


def per_device(lagged_block_entries, pattern, diagonal_block_inverses, excitation, history):
    lags, groups = lax.axis_size("delay"), lax.axis_size("surface")
    lag, position = lax.axis_index("delay"), lax.axis_index("surface")
    core, pair, pairs = lag % 2, lag // 2, lags // 2
    entries = lagged_block_entries[0]
    blocks, slots, size, _ = entries.shape
    steps, rows, columns = excitation.shape

    def device(d, s):
        return d * groups + s

    def everyone(move):
        return [
            (device(d, s), device(*move(d, s))) for d in range(lags) for s in range(groups)
        ]

    def swapped(value):
        return lax.ppermute(value, AXES, everyone(lambda d, s: (d ^ 1, s)))

    def pair_moved(value, hop):
        return lax.ppermute(value, AXES, everyone(lambda d, s: ((d + 2 * hop) % lags, s)))

    def halo(value, hop):
        return lax.ppermute(
            value, AXES, everyone(lambda d, s: (d, (s + (hop if d % 2 == 0 else -hop)) % groups))
        )

    other_history = swapped(history[0])
    even_history = jnp.where(core == 0, history[0], other_history)
    odd_history = jnp.where(core == 0, other_history, history[0])

    span = list(range(blocks))
    half = blocks // 2
    before = [blocks + j for j in span] + span + [2 * blocks + j for j in span[:half]]
    after = (
        [3 * blocks + j for j in span]
        + [4 * blocks + j for j in span]
        + [2 * blocks + j for j in span[half:]]
    )
    order = jnp.where(
        core == 0,
        jnp.array(before + after, jnp.int32),
        jnp.array(after + before, jnp.int32),
    )
    local = (pattern[0] - (position - 2) * blocks) % (blocks * groups)
    match = local[:, :, None] == order[None, None, :]
    slot = jnp.min(
        jnp.where(match, jnp.arange(slots, dtype=jnp.int32)[None, :, None], slots), axis=1
    )
    kept, sent = spread(entries, slot)
    got = swapped(sent)
    near = jnp.where(core == 0, kept, got)
    far = jnp.where(core == 0, got, kept)

    def flags(step):
        return jnp.stack(
            [
                core,
                pair,
                (pair == step - (steps - 1)).astype(jnp.int32),
                (pair == pairs - 1).astype(jnp.int32),
                ((pair == step) | (pair == step + 1)).astype(jnp.int32),
            ]
        ).astype(jnp.int32)

    field_shape = jax.ShapeDtypeStruct((rows, columns), F32)
    current_shape = jax.ShapeDtypeStruct((rows, columns), BF16)
    unit = 2 * rows * columns
    (current,) = call(
        start_body,
        (current_shape,),
        unit * size,
        [flags(0), diagonal_block_inverses, excitation[0], even_history],
    )
    field = jnp.zeros((rows, columns), BF16)
    seen = []
    previous = None
    result = jnp.zeros((rows, columns), F32)
    for step in range(steps + pairs - 1):
        seen.append(current)
        mark = flags(step)
        first, second = halo(current, 1), halo(current, 2)
        if pairs == 2:
            current_in = field_in = pair_moved(jnp.where(pair == 0, current, field), 1)
        else:
            current_in, field_in = pair_moved(current, 1), pair_moved(field, -1)
        if previous is None:
            (early,) = call(
                early_first_body, (field_shape,), unit * rows // 2, [mark, near, current]
            )
        else:
            (early,) = call(
                early_body, (field_shape,), unit * rows * 3, [mark, near, far, current, *previous]
            )
        if step < steps - 1:
            (mine,) = call(
                late_body, (field_shape,), unit * rows * 2, [mark, near, first, second, early]
            )
            other = swapped(mine)
        else:
            mine, send = call(
                late_final_body,
                (field_shape, field_shape),
                unit * rows * 5,
                [mark, near, far, current, first, second, early],
            )
            other = swapped(send)
        came = jnp.where(pair == pairs - 1, 0.0, field_in.astype(F32))
        if step >= steps - 1:
            last = pair == step - (steps - 1)
            result = jnp.where(last, mine + other + jnp.where(core == 0, came, 0.0), result)
            result = jnp.where(
                (core == 1) & (pair == step - steps), result + came, result
            )
        previous = (first, second, current)
        if step < steps + pairs - 2:
            special = step < pairs
            extra = []
            if special:
                extra = [jnp.where(pair == step, odd_history, even_history)]
            current, field = call(
                functools.partial(next_body, special),
                (current_shape, current_shape),
                unit * size,
                [
                    mark,
                    diagonal_block_inverses,
                    excitation[min(step + 1, steps - 1)],
                    mine,
                    other,
                    field_in,
                    current_in,
                ]
                + extra,
            )
    out = []
    for step in range(steps):
        value = seen[step]
        for later in range(1, pairs):
            value = jnp.where(pair == later, seen[step + later], value)
        out.append(value)
    return (jnp.stack(out), result[None])


def solution(mesh):
    placed = (
        P("delay", "surface", None, None, None),
        P("delay", "surface", None),
        P("surface", None, None),
        P(None, "surface", None),
        P("delay", "surface", None),
    )
    return jax.shard_map(
        per_device,
        mesh=mesh,
        in_specs=placed,
        out_specs=(P(None, "surface", None), P("delay", "surface", None)),
        check_vma=False,
    )
```

```python
import functools

import jax
import jax.numpy as jnp
from jax import lax
from jax.experimental import pallas as pl
from jax.experimental.pallas import tpu as pltpu
from jax.sharding import PartitionSpec as P

F32 = jnp.float32
BF16 = jnp.bfloat16
AXES = ("delay", "surface")
VMEM = pl.BlockSpec(memory_space=pltpu.VMEM)
MIB = 1024 * 1024


def dot(a, b):
    return jnp.dot(a, b, preferred_element_type=F32)


def place():
    lag = lax.axis_index("delay")
    return lax.rem(lag, 2), lax.div(lag, 2)


def call(body, outs, flops, args):
    moved = sum(a.size * a.dtype.itemsize for a in args)
    return pl.pallas_call(
        body,
        out_shape=tuple(outs),
        in_specs=[VMEM] * len(args),
        out_specs=tuple(VMEM for _ in outs),
        cost_estimate=pl.CostEstimate(flops=flops, bytes_accessed=moved, transcendentals=0),
        compiler_params=pltpu.CompilerParams(vmem_limit_bytes=8 * MIB),
    )(*args)


def spread_body(groups, pattern_ref, entries_ref, after_ref, keep_ref, send_ref):
    del after_ref
    core, _ = place()
    row = pl.program_id(0)
    blocks = pl.num_programs(0)
    slots, size = entries_ref.shape[1], entries_ref.shape[2]
    total = blocks * groups
    base = (lax.axis_index("surface") - 2) * blocks
    keep_ref[...] = jnp.zeros_like(keep_ref)
    send_ref[...] = jnp.zeros_like(send_ref)
    for slot in range(slots):
        j = lax.rem(pattern_ref[row, slot] - base + total, total)
        first = j < 2 * blocks + blocks // 2
        column = jnp.where(
            j < blocks,
            j + blocks,
            jnp.where(
                j < 2 * blocks,
                j - blocks,
                jnp.where(first, j, jnp.where(j < 3 * blocks, j - blocks // 2, j - 3 * blocks)),
            ),
        )
        columns = pl.ds(pl.multiple_of(column * size, size), size)
        mine = first == (core == 0)

        @pl.when(mine)
        def _():
            keep_ref[:, columns] = entries_ref[0, slot]

        @pl.when(jnp.logical_not(mine))
        def _():
            send_ref[:, columns] = entries_ref[0, slot]


def spread(entries, pattern, groups, after):
    blocks, slots, size, _ = entries.shape
    width = (2 * blocks + blocks // 2) * size
    out = jax.ShapeDtypeStruct((blocks * size, width), entries.dtype)
    return pl.pallas_call(
        functools.partial(spread_body, groups),
        grid_spec=pltpu.PrefetchScalarGridSpec(
            num_scalar_prefetch=1,
            grid=(blocks,),
            in_specs=[
                pl.BlockSpec((1, slots, size, size), lambda i, s: (i, 0, 0, 0)),
                pl.BlockSpec(memory_space=pl.ANY),
            ],
            out_specs=[pl.BlockSpec((size, width), lambda i, s: (i, 0))] * 2,
        ),
        out_shape=(out, out),
        compiler_params=pltpu.CompilerParams(vmem_limit_bytes=8 * MIB),
    )(pattern, entries, after)


def own_half(current_ref):
    core, _ = place()
    rows = current_ref.shape[0] // 2
    return current_ref[pl.ds(pl.multiple_of(core * rows, rows), rows), :]


def early_body(near_ref, far_ref, now_ref, first_ref, second_ref, before_ref, out_ref):
    rows = now_ref.shape[0]
    out_ref[...] = (
        dot(near_ref[:, 2 * rows :], own_half(now_ref))
        + dot(far_ref[:, :rows], first_ref[...])
        + dot(far_ref[:, rows : 2 * rows], second_ref[...])
        + dot(far_ref[:, 2 * rows :], own_half(before_ref))
    )


def early_first_body(near_ref, now_ref, out_ref):
    rows = now_ref.shape[0]
    out_ref[...] = dot(near_ref[:, 2 * rows :], own_half(now_ref))


def came(step, pairs, field_ref, history):
    core, pair = place()
    value = 0.0
    if step > 0:
        value = jnp.where(pair == pairs - 1, 0.0, field_ref[...].astype(F32))
    if history:
        odd_ref, even_ref = history
        value = jnp.where(
            pair == step, odd_ref[...], jnp.where(pair == step + 1, even_ref[...], value)
        )
    return jnp.where(core == 0, value, 0.0)


def late_body(step, pairs, near_ref, first_ref, second_ref, early_ref, field_ref, *rest):
    *history, out_ref = rest
    rows = first_ref.shape[0]
    out_ref[...] = (
        early_ref[...]
        + came(step, pairs, field_ref, history)
        + dot(near_ref[:, :rows], first_ref[...])
        + dot(near_ref[:, rows : 2 * rows], second_ref[...])
    )


def late_final_body(
    step, steps, pairs, near_ref, first_ref, second_ref, early_ref, field_ref, far_ref, now_ref, *rest
):
    *history, keep_ref, send_ref = rest
    core, pair = place()
    rows = first_ref.shape[0]
    even = (
        early_ref[...]
        + came(step, pairs, field_ref, history)
        + dot(near_ref[:, :rows], first_ref[...])
        + dot(near_ref[:, rows : 2 * rows], second_ref[...])
    )
    odd = (
        dot(far_ref[:, :rows], first_ref[...])
        + dot(far_ref[:, rows : 2 * rows], second_ref[...])
        + dot(far_ref[:, 2 * rows :], own_half(now_ref))
    )
    ends = pair == step - (steps - 1)
    keep_ref[...] = jnp.where(jnp.logical_and(ends, core == 1), odd, even)
    send_ref[...] = jnp.where(jnp.logical_and(ends, core == 0), odd, even)


def solve(inverse_ref, rhs, out_ref, keep, other):
    size = inverse_ref.shape[1]
    fresh = []
    for i in range(inverse_ref.shape[0]):
        rows = slice(i * size, (i + 1) * size)
        block = dot(inverse_ref[i], rhs[rows]).astype(BF16)
        fresh.append(jnp.where(keep, block, other[rows]))
        out_ref[rows, :] = fresh[-1]
    return fresh


def start_body(inverse_ref, excitation_ref, history_ref, out_ref):
    _, pair = place()
    rhs = (excitation_ref[...].astype(F32) - history_ref[...]).astype(BF16)
    solve(inverse_ref, rhs, out_ref, pair == 0, jnp.zeros_like(rhs))


def next_body(pairs, inverse_ref, excitation_ref, mine_ref, other_ref, came_ref, out_ref, field_ref):
    _, pair = place()
    field = mine_ref[...] + other_ref[...]
    rhs = (excitation_ref[...].astype(F32) - field).astype(BF16)
    first_pair = pair == 0
    fresh = solve(inverse_ref, rhs, out_ref, first_pair, came_ref)
    if pairs == 2:
        size = inverse_ref.shape[1]
        for i, block in enumerate(fresh):
            rows = slice(i * size, (i + 1) * size)
            field_ref[rows, :] = jnp.where(first_pair, block, field[rows].astype(BF16))
    else:
        field_ref[...] = field.astype(BF16)


def per_device(lagged_block_entries, pattern, diagonal_block_inverses, excitation, history):
    lags, groups = lax.axis_size("delay"), lax.axis_size("surface")
    core, pair = place()
    pairs = lags // 2
    entries = lagged_block_entries[0]
    blocks, slots, size, _ = entries.shape
    steps, rows, columns = excitation.shape

    def device(d, s):
        return d * groups + s

    def everyone(move):
        return [
            (device(d, s), device(*move(d, s))) for d in range(lags) for s in range(groups)
        ]

    def swapped(value):
        return lax.ppermute(value, AXES, everyone(lambda d, s: (d ^ 1, s)))

    def pair_moved(value, hop):
        return lax.ppermute(value, AXES, everyone(lambda d, s: ((d + 2 * hop) % lags, s)))

    def halo(value, hop):
        return lax.ppermute(
            value, AXES, everyone(lambda d, s: (d, (s + (hop if d % 2 == 0 else -hop)) % groups))
        )

    other_history = swapped(history[0])
    even_history = jnp.where(core == 0, history[0], other_history)
    odd_history = jnp.where(core == 0, other_history, history[0])

    field_shape = jax.ShapeDtypeStruct((rows, columns), F32)
    current_shape = jax.ShapeDtypeStruct((rows, columns), BF16)
    unit = 2 * rows * columns
    (current,) = call(
        start_body,
        [current_shape],
        unit * size,
        [diagonal_block_inverses, excitation[0], even_history],
    )
    kept, sent = spread(entries, pattern[0], groups, current)
    got = swapped(sent)
    near = jnp.where(core == 0, kept, got)
    far = jnp.where(core == 0, got, kept)

    going = current
    seen = []
    previous = None
    result = jnp.zeros((rows, columns), F32)
    for step in range(steps + pairs - 1):
        seen.append(current)
        first, second = halo(current, 1), halo(current, 2)
        if pairs == 2:
            current_in = field_in = pair_moved(going, 1)
        else:
            current_in, field_in = pair_moved(current, 1), pair_moved(going, -1)
        if previous is None:
            (early,) = call(early_first_body, [field_shape], unit * rows // 2, [near, current])
        else:
            (early,) = call(
                early_body, [field_shape], unit * rows * 3, [near, far, current, *previous]
            )
        received = [near, first, second, early, field_in]
        extra = [odd_history, even_history] if step < pairs else []
        if step < steps - 1:
            (mine,) = call(
                functools.partial(late_body, step, pairs),
                [field_shape],
                unit * rows * 2,
                received + extra,
            )
            other = swapped(mine)
            came_in = current_in
            current, going = call(
                functools.partial(next_body, pairs),
                [current_shape, current_shape],
                unit * size,
                [diagonal_block_inverses, excitation[step + 1], mine, other, came_in],
            )
        else:
            mine, send = call(
                functools.partial(late_final_body, step, steps, pairs),
                [field_shape, field_shape],
                unit * rows * 5,
                received + [far, current] + extra,
            )
            field = mine + swapped(send)
            last_in = jnp.where(pair == pairs - 1, 0.0, field_in.astype(F32))
            result = jnp.where(pair == step - (steps - 1), field, result)
            result = jnp.where((core == 1) & (pair == step - steps), result + last_in, result)
            previous = (first, second, current)
            current, going = current_in, field.astype(BF16)
        previous = (first, second, seen[-1])
    out = []
    for step in range(steps):
        value = seen[step]
        for later in range(1, pairs):
            value = jnp.where(pair == later, seen[step + later], value)
        out.append(value)
    return (jnp.stack(out), result[None])


def solution(mesh):
    placed = (
        P("delay", "surface", None, None, None),
        P("delay", "surface", None),
        P("surface", None, None),
        P(None, "surface", None),
        P("delay", "surface", None),
    )
    return jax.shard_map(
        per_device,
        mesh=mesh,
        in_specs=placed,
        out_specs=(P(None, "surface", None), P("delay", "surface", None)),
        check_vma=False,
    )
```

```python
import functools

import jax
import jax.numpy as jnp
from jax import lax
from jax.experimental import pallas as pl
from jax.experimental.pallas import tpu as pltpu
from jax.sharding import PartitionSpec as P

F32 = jnp.float32
BF16 = jnp.bfloat16
AXES = ("delay", "surface")
VMEM = pl.BlockSpec(memory_space=pltpu.VMEM)
MIB = 1024 * 1024


def dot(a, b):
    return jnp.dot(a, b, preferred_element_type=F32)


def place():
    lag = lax.axis_index("delay")
    return lax.rem(lag, 2), lax.div(lag, 2)


COST = pl.CostEstimate(flops=1, bytes_accessed=1, transcendentals=0)


def call(body, outs, args):
    return pl.pallas_call(
        body,
        out_shape=tuple(outs),
        in_specs=[VMEM] * len(args),
        out_specs=tuple(VMEM for _ in outs),
        cost_estimate=COST,
        compiler_params=pltpu.CompilerParams(vmem_limit_bytes=8 * MIB),
    )(*args)


def choose(*cases):
    *pairs, value = cases
    for when, other in reversed(pairs):
        value = jnp.where(when, other, value)
    return value


def far_next(s, count):
    return choose((s == 0, count - 2), (s == 1, count - 1), (s == count - 1, 0), s - 1)


def far_last(s, count):
    return choose((s == 0, count - 1), (s == count - 2, 0), (s == count - 1, 1), s + 1)


def close_next(s, count):
    even = lax.rem(s, 2) == 0
    return choose((s == 1, 0), (s == count - 2, count - 1), (even, s + 2), s - 2)


def close_last(s, count):
    even = lax.rem(s, 2) == 0
    return choose((s == 0, 1), (s == count - 1, count - 2), (even, s - 2), s + 2)


def tour(far, count):
    if far:
        return [0] + list(range(count - 2, 0, -1)) + [count - 1]
    return list(range(0, count, 2)) + list(range(count - 1, 0, -2))


def spread_body(groups, pattern_ref, entries_ref, out_ref):
    core, _ = place()
    row = pl.program_id(0)
    blocks = pl.num_programs(0)
    slots, size = entries_ref.shape[1], entries_ref.shape[2]
    here = lax.axis_index("surface")
    brought = (
        (far_last(here, groups), 0, 0),
        (close_last(here, groups), 0, blocks),
        (far_next(here, groups), 1, 0),
        (close_next(here, groups), 1, blocks),
    )
    out_ref[...] = jnp.zeros_like(out_ref)
    for slot in range(slots):
        block = pattern_ref[row, slot]
        group = lax.div(block, blocks)
        within = block - group * blocks
        second = within >= blocks // 2
        half = jnp.where(second, 1, 0)
        column = 2 * blocks + jnp.where(second, within - blocks // 2, within)
        for source, side, first in brought:
            half = jnp.where(group == source, side, half)
            column = jnp.where(group == source, first + within, column)
        columns = pl.ds(pl.multiple_of(column * size, size), size)
        out_ref[jnp.where(half == core, 0, 1), :, columns] = entries_ref[0, slot]


def spread(entries, pattern, groups):
    blocks, slots, size, _ = entries.shape
    width = (2 * blocks + blocks // 2) * size
    return pl.pallas_call(
        functools.partial(spread_body, groups),
        grid_spec=pltpu.PrefetchScalarGridSpec(
            num_scalar_prefetch=1,
            grid=(blocks,),
            in_specs=[pl.BlockSpec((1, slots, size, size), lambda i, s: (i, 0, 0, 0))],
            out_specs=pl.BlockSpec((2, size, width), lambda i, s: (0, i, 0)),
        ),
        out_shape=jax.ShapeDtypeStruct((2, blocks * size, width), entries.dtype),
        cost_estimate=COST,
        compiler_params=pltpu.CompilerParams(vmem_limit_bytes=8 * MIB),
    )(pattern, entries)


def own_half(current_ref):
    core, _ = place()
    rows = current_ref.shape[0] // 2
    return current_ref[pl.ds(pl.multiple_of(core * rows, rows), rows), :]


def early_body(near_ref, second_ref, now_ref, *rest):
    *last, out_ref = rest
    rows = now_ref.shape[0]
    total = dot(near_ref[:, rows : 2 * rows], second_ref[...])
    total += dot(near_ref[:, 2 * rows :], own_half(now_ref))
    if last:
        far_ref, first_ref, second_ref, before_ref = last
        total += dot(far_ref[:, :rows], first_ref[...])
        total += dot(far_ref[:, rows : 2 * rows], second_ref[...])
        total += dot(far_ref[:, 2 * rows :], own_half(before_ref))
    out_ref[...] = total


def came(step, pairs, field_ref, history):
    core, pair = place()
    value = 0.0
    if step > 0:
        value = jnp.where(pair == pairs - 1, 0.0, field_ref[...].astype(F32))
    if history:
        odd_ref, even_ref = history
        value = jnp.where(
            pair == step, odd_ref[...], jnp.where(pair == step + 1, even_ref[...], value)
        )
    return jnp.where(core == 0, value, 0.0)


def late_body(step, pairs, near_ref, first_ref, early_ref, field_ref, *rest):
    *history, out_ref = rest
    rows = first_ref.shape[0]
    out_ref[...] = (
        early_ref[...]
        + came(step, pairs, field_ref, history)
        + dot(near_ref[:, :rows], first_ref[...])
    )


def late_final_body(
    step, steps, pairs, near_ref, first_ref, early_ref, field_ref, far_ref, second_ref, now_ref, *rest
):
    *history, keep_ref, send_ref = rest
    core, pair = place()
    rows = first_ref.shape[0]
    even = (
        early_ref[...]
        + came(step, pairs, field_ref, history)
        + dot(near_ref[:, :rows], first_ref[...])
    )
    odd = (
        dot(far_ref[:, :rows], first_ref[...])
        + dot(far_ref[:, rows : 2 * rows], second_ref[...])
        + dot(far_ref[:, 2 * rows :], own_half(now_ref))
    )
    ends = pair == step - (steps - 1)
    keep_ref[...] = jnp.where(jnp.logical_and(ends, core == 1), odd, even)
    send_ref[...] = jnp.where(jnp.logical_and(ends, core == 0), odd, even)


def solve(inverse_ref, rhs, out_ref, keep, other):
    size = inverse_ref.shape[1]
    fresh = []
    for i in range(inverse_ref.shape[0]):
        rows = slice(i * size, (i + 1) * size)
        block = dot(inverse_ref[i], rhs[rows]).astype(BF16)
        fresh.append(jnp.where(keep, block, other[rows]))
        out_ref[rows, :] = fresh[-1]
    return fresh


def start_body(inverse_ref, excitation_ref, history_ref, out_ref):
    _, pair = place()
    rhs = (excitation_ref[0].astype(F32) - history_ref[...]).astype(BF16)
    solve(inverse_ref, rhs, out_ref, pair == 0, jnp.zeros_like(rhs))


def next_body(step, pairs, inverse_ref, excitation_ref, mine_ref, other_ref, came_ref, out_ref, field_ref):
    _, pair = place()
    field = mine_ref[...] + other_ref[...]
    rhs = (excitation_ref[step + 1].astype(F32) - field).astype(BF16)
    first_pair = pair == 0
    fresh = solve(inverse_ref, rhs, out_ref, first_pair, came_ref)
    if pairs == 2:
        size = inverse_ref.shape[1]
        for i, block in enumerate(fresh):
            rows = slice(i * size, (i + 1) * size)
            field_ref[rows, :] = jnp.where(first_pair, block, field[rows].astype(BF16))
    else:
        field_ref[...] = field.astype(BF16)


def per_device(lagged_block_entries, pattern, diagonal_block_inverses, excitation, history):
    lags, groups = lax.axis_size("delay"), lax.axis_size("surface")
    core, pair = place()
    pairs = lags // 2
    entries = lagged_block_entries[0]
    blocks, slots, size, _ = entries.shape
    steps, rows, columns = excitation.shape

    def device(d, s):
        return d * groups + s

    def everyone(move):
        return [
            (device(d, s), device(*move(d, s))) for d in range(lags) for s in range(groups)
        ]

    def swapped(value):
        return lax.ppermute(value, AXES, everyone(lambda d, s: (d ^ 1, s)))

    def pair_moved(value, hop):
        return lax.ppermute(value, AXES, everyone(lambda d, s: ((d + 2 * hop) % lags, s)))

    def halo(value, far):
        order = tour(far, groups)
        following = dict(zip(order, order[1:] + order[:1]))
        preceding = {t: s for s, t in following.items()}
        return lax.ppermute(
            value,
            AXES,
            everyone(lambda d, s: (d, following[s] if d % 2 == 0 else preceding[s])),
        )

    other_history = swapped(history[0])
    even_history = jnp.where(core == 0, history[0], other_history)
    odd_history = jnp.where(core == 0, other_history, history[0])

    field_shape = jax.ShapeDtypeStruct((rows, columns), F32)
    current_shape = jax.ShapeDtypeStruct((rows, columns), BF16)
    (current,) = call(
        start_body, [current_shape], [diagonal_block_inverses, excitation, even_history]
    )
    both = spread(entries, pattern[0], groups)
    kept, got = both[0], swapped(both[1])
    near = jnp.where(core == 0, kept, got)
    far = jnp.where(core == 0, got, kept)

    going = current
    seen = []
    previous = None
    result = jnp.zeros((rows, columns), F32)
    for step in range(steps + pairs - 1):
        seen.append(current)
        first, second = halo(current, True), halo(current, False)
        if pairs == 2:
            current_in = field_in = pair_moved(going, 1)
        else:
            current_in, field_in = pair_moved(current, 1), pair_moved(going, -1)
        last = [far, *previous] if previous else []
        (early,) = call(early_body, [field_shape], [near, second, current] + last)
        received = [near, first, early, field_in]
        extra = [odd_history, even_history] if step < pairs else []
        previous = (first, second, current)
        if step < steps - 1:
            (mine,) = call(
                functools.partial(late_body, step, pairs), [field_shape], received + extra
            )
            current, going = call(
                functools.partial(next_body, step, pairs),
                [current_shape, current_shape],
                [diagonal_block_inverses, excitation, mine, swapped(mine), current_in],
            )
        else:
            mine, send = call(
                functools.partial(late_final_body, step, steps, pairs),
                [field_shape, field_shape],
                received + [far, second, current] + extra,
            )
            field = mine + swapped(send)
            last_in = jnp.where(pair == pairs - 1, 0.0, field_in.astype(F32))
            result = jnp.where(pair == step - (steps - 1), field, result)
            result = jnp.where((core == 1) & (pair == step - steps), result + last_in, result)
            current, going = current_in, field.astype(BF16)
    out = []
    for step in range(steps):
        value = seen[step]
        for later in range(1, pairs):
            value = jnp.where(pair == later, seen[step + later], value)
        out.append(value)
    return (jnp.stack(out), result[None])


def solution(mesh):
    placed = (
        P("delay", "surface", None, None, None),
        P("delay", "surface", None),
        P("surface", None, None),
        P(None, "surface", None),
        P("delay", "surface", None),
    )
    return jax.shard_map(
        per_device,
        mesh=mesh,
        in_specs=placed,
        out_specs=(P(None, "surface", None), P("delay", "surface", None)),
        check_vma=False,
    )
```

```python
import functools

import jax
import jax.numpy as jnp
from jax import lax
from jax.experimental import pallas as pl
from jax.experimental.pallas import tpu as pltpu
from jax.sharding import PartitionSpec as P

F32 = jnp.float32
BF16 = jnp.bfloat16
AXES = ("delay", "surface")
VMEM = pl.BlockSpec(memory_space=pltpu.VMEM)
MIB = 1024 * 1024


def dot(a, b):
    return jnp.dot(a, b, preferred_element_type=F32)


def place():
    lag = lax.axis_index("delay")
    return lax.rem(lag, 2), lax.div(lag, 2)


def cost(microseconds):
    moved = int(3.6e6 * microseconds)
    return pl.CostEstimate(flops=0, bytes_accessed=moved, transcendentals=0)


def call(body, outs, args, after=None, microseconds=0.5):
    specs = [VMEM] * len(args)
    if after is not None:
        args, specs = [after] + args, [pl.BlockSpec(memory_space=pl.ANY)] + specs
        body = functools.partial(skip_first, body)
    return pl.pallas_call(
        body,
        out_shape=tuple(outs),
        in_specs=specs,
        out_specs=tuple(VMEM for _ in outs),
        cost_estimate=cost(microseconds),
        compiler_params=pltpu.CompilerParams(vmem_limit_bytes=8 * MIB),
    )(*args)


def skip_first(body, _, *refs):
    body(*refs)


def choose(*cases):
    *pairs, value = cases
    for when, other in reversed(pairs):
        value = jnp.where(when, other, value)
    return value


def far_next(s, count):
    return choose((s == 0, count - 2), (s == 1, count - 1), (s == count - 1, 0), s - 1)


def far_last(s, count):
    return choose((s == 0, count - 1), (s == count - 2, 0), (s == count - 1, 1), s + 1)


def close_next(s, count):
    even = lax.rem(s, 2) == 0
    return choose((s == 1, 0), (s == count - 2, count - 1), (even, s + 2), s - 2)


def close_last(s, count):
    even = lax.rem(s, 2) == 0
    return choose((s == 0, 1), (s == count - 1, count - 2), (even, s - 2), s + 2)


def tour(far, count):
    if far:
        return [0] + list(range(count - 2, 0, -1)) + [count - 1]
    return list(range(0, count, 2)) + list(range(count - 1, 0, -2))


def spread_body(groups, pattern_ref, entries_ref, keep_ref, send_ref, here_ref, both_ref, sems):
    core, _ = place()
    blocks, slots, size, _ = entries_ref.shape
    copies = [
        pltpu.make_async_copy(entries_ref.at[row], here_ref.at[row], sems.at[row])
        for row in range(blocks)
    ]
    for copy in copies:
        copy.start()
    here = lax.axis_index("surface")
    brought = (
        (far_last(here, groups), 0, 0),
        (close_last(here, groups), 0, blocks),
        (far_next(here, groups), 1, 0),
        (close_next(here, groups), 1, blocks),
    )
    both_ref[...] = jnp.zeros_like(both_ref)
    for row in range(blocks):
        copies[row].wait()
        rows = slice(row * size, (row + 1) * size)
        for slot in range(slots):
            block = pattern_ref[row, slot]
            group = lax.div(block, blocks)
            within = block - group * blocks
            second = within >= blocks // 2
            half = jnp.where(second, 1, 0)
            column = 2 * blocks + jnp.where(second, within - blocks // 2, within)
            for source, side, first in brought:
                half = jnp.where(group == source, side, half)
                column = jnp.where(group == source, first + within, column)
            columns = pl.ds(pl.multiple_of(column * size, size), size)
            both_ref[jnp.where(half == core, 0, 1), rows, columns] = here_ref[row, slot]
        keep_ref[rows, :] = both_ref[0, rows, :]
        send_ref[rows, :] = both_ref[1, rows, :]


def spread(entries, pattern, groups):
    blocks, slots, size, _ = entries.shape
    shape = (blocks * size, (2 * blocks + blocks // 2) * size)
    out = jax.ShapeDtypeStruct(shape, entries.dtype)
    return pl.pallas_call(
        functools.partial(spread_body, groups),
        out_shape=(out, out),
        in_specs=[
            pl.BlockSpec(memory_space=pltpu.SMEM),
            pl.BlockSpec(memory_space=pltpu.HBM),
        ],
        out_specs=(VMEM, VMEM),
        scratch_shapes=[
            pltpu.VMEM(entries.shape, entries.dtype),
            pltpu.VMEM((2, *shape), entries.dtype),
            pltpu.SemaphoreType.DMA((blocks,)),
        ],
        cost_estimate=cost(4),
        compiler_params=pltpu.CompilerParams(vmem_limit_bytes=12 * MIB),
    )(pattern, entries)


def arrange_body(kept_ref, got_ref, near_ref, far_ref):
    core, _ = place()

    @pl.when(core == 0)
    def _():
        near_ref[...] = kept_ref[...]
        far_ref[...] = got_ref[...]

    @pl.when(core == 1)
    def _():
        near_ref[...] = got_ref[...]
        far_ref[...] = kept_ref[...]


def own_half(current_ref):
    core, _ = place()
    rows = current_ref.shape[0] // 2
    return current_ref[pl.ds(pl.multiple_of(core * rows, rows), rows), :]


def early_body(near_ref, now_ref, *rest):
    *last, out_ref = rest
    rows = now_ref.shape[0]
    total = dot(near_ref[:, 2 * rows :], own_half(now_ref))
    if last:
        far_ref, first_ref, second_ref, before_ref = last
        total += dot(far_ref[:, :rows], first_ref[...])
        total += dot(far_ref[:, rows : 2 * rows], second_ref[...])
        total += dot(far_ref[:, 2 * rows :], own_half(before_ref))
    out_ref[...] = total


def late_sum(step, pairs, near_ref, first_ref, second_ref, early_ref, field):
    core, pair = place()
    rows = first_ref.shape[0]
    total = early_ref[...]
    total += dot(near_ref[:, :rows], first_ref[...])
    total += dot(near_ref[:, rows : 2 * rows], second_ref[...])
    if not field:
        return total
    field_ref, *history = field
    value = jnp.where(pair == pairs - 1, 0.0, field_ref[...].astype(F32))
    if history:
        mine_ref, other_ref = history
        value = jnp.where(
            pair == step, other_ref[...], jnp.where(pair == step + 1, mine_ref[...], value)
        )
    return total + jnp.where(core == 0, value, 0.0)


def late_body(step, pairs, near_ref, first_ref, second_ref, early_ref, *rest):
    *field, out_ref = rest
    out_ref[...] = late_sum(step, pairs, near_ref, first_ref, second_ref, early_ref, field)


def late_final_body(
    step, steps, pairs, near_ref, first_ref, second_ref, early_ref, far_ref, now_ref, *rest
):
    *field, keep_ref, send_ref = rest
    core, pair = place()
    rows = first_ref.shape[0]
    even = late_sum(step, pairs, near_ref, first_ref, second_ref, early_ref, field)
    odd = (
        dot(far_ref[:, :rows], first_ref[...])
        + dot(far_ref[:, rows : 2 * rows], second_ref[...])
        + dot(far_ref[:, 2 * rows :], own_half(now_ref))
    )
    ends = pair == step - (steps - 1)
    keep_ref[...] = jnp.where(jnp.logical_and(ends, core == 1), odd, even)
    send_ref[...] = jnp.where(jnp.logical_and(ends, core == 0), odd, even)


def finish_body(step, steps, mine_ref, other_ref, *rest):
    *earlier, result_ref, field_ref = rest
    core, pair = place()
    field = mine_ref[...] + other_ref[...]
    field_ref[...] = field.astype(BF16)
    if earlier:
        before_ref, field_in_ref = earlier
        adds = jnp.logical_and(core == 1, pair == step - steps)
        before = before_ref[...] + jnp.where(adds, field_in_ref[...].astype(F32), 0.0)
        field = jnp.where(pair == step - (steps - 1), field, before)
    result_ref[...] = field


def collect_body(pairs, *refs):
    *seen, out_ref = refs
    _, pair = place()
    for step in range(out_ref.shape[0]):
        value = seen[step][...]
        for later in range(1, pairs):
            value = jnp.where(pair == later, seen[step + later][...], value)
        out_ref[step] = value


def solve(inverse_ref, rhs, out_ref, keep, other):
    size = inverse_ref.shape[1]
    fresh = []
    for i in range(inverse_ref.shape[0]):
        rows = slice(i * size, (i + 1) * size)
        block = dot(inverse_ref[i], rhs[rows]).astype(BF16)
        fresh.append(jnp.where(keep, block, other[rows]))
        out_ref[rows, :] = fresh[-1]
    return fresh


def start_body(inverse_ref, excitation_ref, history_ref, other_history_ref, out_ref):
    core, pair = place()
    history = jnp.where(core == 0, history_ref[...], other_history_ref[...])
    rhs = (excitation_ref[0].astype(F32) - history).astype(BF16)
    solve(inverse_ref, rhs, out_ref, pair == 0, jnp.zeros_like(rhs))


def next_body(step, pairs, inverse_ref, excitation_ref, mine_ref, other_ref, came_ref, out_ref, field_ref):
    _, pair = place()
    field = mine_ref[...] + other_ref[...]
    rhs = (excitation_ref[step + 1].astype(F32) - field).astype(BF16)
    first_pair = pair == 0
    fresh = solve(inverse_ref, rhs, out_ref, first_pair, came_ref)
    if pairs == 2:
        size = inverse_ref.shape[1]
        for i, block in enumerate(fresh):
            rows = slice(i * size, (i + 1) * size)
            field_ref[rows, :] = jnp.where(first_pair, block, field[rows].astype(BF16))
    else:
        field_ref[...] = field.astype(BF16)


def per_device(lagged_block_entries, pattern, diagonal_block_inverses, excitation, history):
    lags, groups = lax.axis_size("delay"), lax.axis_size("surface")
    pairs = lags // 2
    entries = lagged_block_entries[0]
    blocks, slots, size, _ = entries.shape
    steps, rows, columns = excitation.shape

    def device(d, s):
        return d * groups + s

    def everyone(move):
        return [
            (device(d, s), device(*move(d, s))) for d in range(lags) for s in range(groups)
        ]

    def swapped(value):
        return lax.ppermute(value, AXES, everyone(lambda d, s: (d ^ 1, s)))

    def pair_moved(value, hop):
        return lax.ppermute(value, AXES, everyone(lambda d, s: ((d + 2 * hop) % lags, s)))

    def halo(value, far):
        order = tour(far, groups)
        following = dict(zip(order, order[1:] + order[:1]))
        preceding = {t: s for s, t in following.items()}
        return lax.ppermute(
            value,
            AXES,
            everyone(lambda d, s: (d, following[s] if d % 2 == 0 else preceding[s])),
        )

    other_history = swapped(history[0])
    field_shape = jax.ShapeDtypeStruct((rows, columns), F32)
    current_shape = jax.ShapeDtypeStruct((rows, columns), BF16)
    kept, sent = spread(entries, pattern[0], groups)
    (current,) = call(
        start_body,
        [current_shape],
        [diagonal_block_inverses, excitation, history[0], other_history],
        after=kept,
    )
    matrix_shape = jax.ShapeDtypeStruct(kept.shape, kept.dtype)
    near, far = call(arrange_body, [matrix_shape, matrix_shape], [kept, swapped(sent)])

    going = current
    seen = []
    previous = []
    result = []
    out = None
    rounds = steps + pairs - 1
    for step in range(rounds):
        seen.append(current)
        if step == rounds - 1:
            (out,) = call(
                functools.partial(collect_body, pairs),
                [jax.ShapeDtypeStruct(excitation.shape, BF16)],
                seen,
            )
        first, second = halo(current, True), halo(current, False)
        if pairs == 2:
            current_in = field_in = pair_moved(going, 1)
        else:
            current_in, field_in = pair_moved(current, 1), pair_moved(going, -1)
        last = [far, *previous] if previous else []
        (early,) = call(early_body, [field_shape], [near, current] + last)
        received = [near, first, second, early]
        field = [field_in] if step < rounds - 1 else []
        if step < pairs:
            field += [history[0], other_history]
        previous = [first, second, current]
        if step < steps - 1:
            (mine,) = call(
                functools.partial(late_body, step, pairs), [field_shape], received + field
            )
            current, going = call(
                functools.partial(next_body, step, pairs),
                [current_shape, current_shape],
                [diagonal_block_inverses, excitation, mine, swapped(mine), current_in],
            )
        else:
            mine, send = call(
                functools.partial(late_final_body, step, steps, pairs),
                [field_shape, field_shape],
                received + [far, current] + field,
                after=out,
                microseconds=0.5 if out is None else 20,
            )
            result, going = call(
                functools.partial(finish_body, step, steps),
                [field_shape, current_shape],
                [mine, swapped(send)] + ([result, field_in] if step >= steps else []),
            )
            current = current_in
    return (out, result[None])


def solution(mesh):
    placed = (
        P("delay", "surface", None, None, None),
        P("delay", "surface", None),
        P("surface", None, None),
        P(None, "surface", None),
        P("delay", "surface", None),
    )
    return jax.shard_map(
        per_device,
        mesh=mesh,
        in_specs=placed,
        out_specs=(P(None, "surface", None), P("delay", "surface", None)),
        check_vma=False,
    )
```

```python
import functools

import jax
import jax.numpy as jnp
from jax import lax
from jax.experimental import pallas as pl
from jax.experimental.pallas import tpu as pltpu
from jax.sharding import PartitionSpec as P

F32 = jnp.float32
BF16 = jnp.bfloat16
AXES = ("delay", "surface")
VMEM = pl.BlockSpec(memory_space=pltpu.VMEM)
MIB = 1024 * 1024
TOKEN = jax.ShapeDtypeStruct((8, 128), F32)


def dot(a, b):
    return jnp.dot(a, b, preferred_element_type=F32)


def place():
    lag = lax.axis_index("delay")
    return lax.rem(lag, 2), lax.div(lag, 2)


def cost(microseconds):
    moved = int(3.6e6 * microseconds)
    return pl.CostEstimate(flops=0, bytes_accessed=moved, transcendentals=0)


def call(body, outs, args, after=None, microseconds=0.5):
    specs = [VMEM] * len(args)
    if after is not None:
        args, specs = [after] + args, [pl.BlockSpec(memory_space=pl.ANY)] + specs
        body = functools.partial(skip_first, body)
    return pl.pallas_call(
        body,
        out_shape=tuple(outs),
        in_specs=specs,
        out_specs=tuple(VMEM for _ in outs),
        cost_estimate=cost(microseconds),
        compiler_params=pltpu.CompilerParams(vmem_limit_bytes=8 * MIB),
    )(*args)


def skip_first(body, _, *refs):
    body(*refs)


def choose(*cases):
    *pairs, value = cases
    for when, other in reversed(pairs):
        value = jnp.where(when, other, value)
    return value


def far_next(s, count):
    return choose((s == 0, count - 2), (s == 1, count - 1), (s == count - 1, 0), s - 1)


def far_last(s, count):
    return choose((s == 0, count - 1), (s == count - 2, 0), (s == count - 1, 1), s + 1)


def close_next(s, count):
    even = lax.rem(s, 2) == 0
    return choose((s == 1, 0), (s == count - 2, count - 1), (even, s + 2), s - 2)


def close_last(s, count):
    even = lax.rem(s, 2) == 0
    return choose((s == 0, 1), (s == count - 1, count - 2), (even, s - 2), s + 2)


def tour(far, count):
    if far:
        return [0] + list(range(count - 2, 0, -1)) + [count - 1]
    return list(range(0, count, 2)) + list(range(count - 1, 0, -2))


def spread_body(groups, pattern_ref, entries_ref, keep_ref, own_ref, *rest):
    *send_refs, here_ref, all_ref, sems = rest
    core, _ = place()
    blocks, slots, size, _ = entries_ref.shape
    copies = [
        pltpu.make_async_copy(entries_ref.at[row], here_ref.at[row], sems.at[row])
        for row in range(blocks)
    ]
    for copy in copies:
        copy.start()
    here = lax.axis_index("surface")
    brought = (
        (far_last(here, groups), 0),
        (close_last(here, groups), 1),
        (far_next(here, groups), 2),
        (close_next(here, groups), 3),
    )
    mine = 2 * blocks * core
    all_ref[...] = jnp.zeros_like(all_ref)
    for row in range(blocks):
        copies[row].wait()
        rows = slice(row * size, (row + 1) * size)
        for slot in range(slots):
            block = pattern_ref[row, slot]
            group = lax.div(block, blocks)
            part = 4
            for source, number in brought:
                part = jnp.where(group == source, number, part)
            column = part * blocks + block - group * blocks
            columns = pl.ds(pl.multiple_of(column * size, size), size)
            all_ref[rows, columns] = here_ref[row, slot]
        width = 2 * blocks * size
        first = pl.ds(pl.multiple_of(core * width, width), width)
        second = pl.ds(pl.multiple_of((1 - core) * width, width), width)
        keep_ref[rows, :] = all_ref[rows, first]
        send_refs[row][...] = all_ref[rows, second]
        own_ref[rows, :] = all_ref[rows, 2 * width :]


def spread(entries, pattern, groups):
    blocks, slots, size, _ = entries.shape
    side = blocks * size

    def matrix(rows, columns):
        return jax.ShapeDtypeStruct((rows, columns), entries.dtype)

    return pl.pallas_call(
        functools.partial(spread_body, groups),
        out_shape=(matrix(side, 2 * side), matrix(side, side), *[matrix(size, 2 * side)] * blocks),
        in_specs=[
            pl.BlockSpec(memory_space=pltpu.SMEM),
            pl.BlockSpec(memory_space=pltpu.HBM),
        ],
        out_specs=(VMEM,) * (blocks + 2),
        scratch_shapes=[
            pltpu.VMEM(entries.shape, entries.dtype),
            pltpu.VMEM((side, 5 * side), entries.dtype),
            pltpu.SemaphoreType.DMA((blocks,)),
        ],
        cost_estimate=cost(4),
        compiler_params=pltpu.CompilerParams(vmem_limit_bytes=54 * MIB),
    )(pattern, entries)


def arrange_body(kept_ref, *rest):
    *got_refs, near_ref, far_ref = rest
    core, _ = place()

    def put(got_to_ref, kept_to_ref):
        kept_to_ref[...] = kept_ref[...]
        for i, got_ref in enumerate(got_refs):
            size = got_ref.shape[0]
            got_to_ref[i * size : (i + 1) * size, :] = got_ref[...]

    @pl.when(core == 0)
    def _():
        put(far_ref, near_ref)

    @pl.when(core == 1)
    def _():
        put(near_ref, far_ref)


def window(matrix_ref, first_ref, second_ref):
    rows = first_ref.shape[0]
    return dot(matrix_ref[:, :rows], first_ref[...]) + dot(matrix_ref[:, rows:], second_ref[...])


def early_body(own_ref, now_ref, *rest):
    *last, out_ref = rest
    core, _ = place()
    if last:
        far_ref, first_ref, second_ref, before_ref = last
        local = jnp.where(core == 0, now_ref[...], before_ref[...])
        out_ref[...] = dot(own_ref[...], local) + window(far_ref, first_ref, second_ref)
    else:
        local = jnp.where(core == 0, now_ref[...], jnp.zeros_like(now_ref))
        out_ref[...] = dot(own_ref[...], local)


def came(step, pairs, field_ref, history):
    core, pair = place()
    value = jnp.where(pair == pairs - 1, 0.0, field_ref[...].astype(F32))
    if history:
        mine_ref, other_ref = history
        past = jnp.where(pair == step, other_ref[...], mine_ref[...])
        special = jnp.logical_or(pair == step, pair == step + 1)
        value = jnp.where(special, jnp.where(core == 0, past, 0.0), value)
    return value


def late_body(step, pairs, near_ref, first_ref, second_ref, early_ref, field_ref, *rest):
    *history, out_ref = rest
    total = early_ref[...] + window(near_ref, first_ref, second_ref)
    out_ref[...] = (total + came(step, pairs, field_ref, history)).astype(BF16)


def last_body(near_ref, first_ref, second_ref, early_ref, far_ref, own_ref, now_ref, even_ref, odd_ref):
    core, _ = place()
    even_ref[...] = early_ref[...] + window(near_ref, first_ref, second_ref)
    local = jnp.where(core == 1, now_ref[...], jnp.zeros_like(now_ref))
    odd_ref[...] = window(far_ref, first_ref, second_ref) + dot(own_ref[...], local)


def share_body(step, steps, pairs, even_ref, odd_ref, field_ref, *rest):
    *history, keep_ref, send_ref, field_out_ref = rest
    core, pair = place()
    even = even_ref[...] + came(step, pairs, field_ref, history)
    odd = odd_ref[...]
    ended = pair == step - steps
    late = field_ref[...].astype(F32)
    keep_ref[...] = jnp.where(ended, late, jnp.where(core == 1, odd, even))
    send_ref[...] = jnp.where(ended, late, jnp.where(core == 0, odd, even)).astype(BF16)
    field_out_ref[...] = even.astype(BF16)


def finish_body(step, steps, mine_ref, other_ref, *rest):
    *earlier, result_ref = rest
    core, pair = place()
    field = mine_ref[...] + other_ref[...].astype(F32)
    if earlier:
        before = earlier[0][...]
        ended = pair == step - steps
        adds = jnp.logical_and(ended, core == 1)
        field = jnp.where(
            adds, before + field, jnp.where(pair == step - (steps - 1), field, before)
        )
    result_ref[...] = field


def collect_body(pairs, *refs):
    *seen, out_ref, token_ref = refs
    token_ref[...] = jnp.zeros_like(token_ref)
    _, pair = place()
    for step in range(out_ref.shape[0]):
        value = seen[step][...]
        for later in range(1, pairs):
            value = jnp.where(pair == later, seen[step + later][...], value)
        out_ref[step] = value


def solve(inverse_ref, rhs, out_ref, keep, other):
    size = inverse_ref.shape[1]
    fresh = []
    for i in range(inverse_ref.shape[0]):
        rows = slice(i * size, (i + 1) * size)
        block = dot(inverse_ref[i], rhs[rows]).astype(BF16)
        fresh.append(jnp.where(keep, block, other[rows]))
        out_ref[rows, :] = fresh[-1]
    return fresh


def first_history_body(history_ref, other_history_ref, out_ref):
    core, _ = place()
    out_ref[...] = jnp.where(core == 0, history_ref[...], other_history_ref[...])


def start_body(inverse_ref, excitation_ref, history_ref, out_ref):
    _, pair = place()
    rhs = (excitation_ref[0].astype(F32) - history_ref[...]).astype(BF16)
    solve(inverse_ref, rhs, out_ref, pair == 0, jnp.zeros_like(rhs))


def next_body(step, inverse_ref, excitation_ref, mine_ref, other_ref, came_ref, out_ref, going_ref):
    _, pair = place()
    field = mine_ref[...].astype(F32) + other_ref[...].astype(F32)
    rhs = (excitation_ref[step + 1].astype(F32) - field).astype(BF16)
    first_pair = pair == 0
    size = inverse_ref.shape[1]
    for i, block in enumerate(solve(inverse_ref, rhs, out_ref, first_pair, came_ref)):
        rows = slice(i * size, (i + 1) * size)
        going_ref[rows, :] = jnp.where(first_pair, block, mine_ref[rows, :])


def per_device(lagged_block_entries, pattern, diagonal_block_inverses, excitation, history):
    lags, groups = lax.axis_size("delay"), lax.axis_size("surface")
    pairs = lags // 2
    entries = lagged_block_entries[0]
    blocks, slots, size, _ = entries.shape
    steps, rows, columns = excitation.shape

    def device(d, s):
        return d * groups + s

    def everyone(move):
        return [
            (device(d, s), device(*move(d, s))) for d in range(lags) for s in range(groups)
        ]

    def swapped(value):
        return lax.ppermute(value, AXES, everyone(lambda d, s: (d ^ 1, s)))

    def pair_moved(value, hop):
        return lax.ppermute(value, AXES, everyone(lambda d, s: ((d + 2 * hop) % lags, s)))

    def halo(value, far):
        order = tour(far, groups)
        following = dict(zip(order, order[1:] + order[:1]))
        preceding = {t: s for s, t in following.items()}
        return lax.ppermute(
            value,
            AXES,
            everyone(lambda d, s: (d, following[s] if d % 2 == 0 else preceding[s])),
        )

    other_history = swapped(history[0])
    field_shape = jax.ShapeDtypeStruct((rows, columns), F32)
    current_shape = jax.ShapeDtypeStruct((rows, columns), BF16)
    kept, own, *sent = spread(entries, pattern[0], groups)
    (first_history,) = call(first_history_body, [field_shape], [history[0], other_history])
    (current,) = call(
        start_body,
        [current_shape],
        [diagonal_block_inverses, excitation, first_history],
    )
    matrix_shape = jax.ShapeDtypeStruct(kept.shape, kept.dtype)
    near, far = call(arrange_body, [matrix_shape, matrix_shape], [kept] + [swapped(part) for part in sent])

    going = field = current
    seen = []
    previous = []
    result = []
    out = collected = None
    rounds = steps + pairs - 1
    windows = None
    for step in range(rounds):
        seen.append(current)
        if step == rounds - 1:
            out, collected = call(
                functools.partial(collect_body, pairs),
                [jax.ShapeDtypeStruct(excitation.shape, BF16), TOKEN],
                seen,
            )
        first, second = windows or (halo(current, True), halo(current, False))
        if pairs == 2:
            current_in = field_in = pair_moved(going, 1)
        else:
            current_in, field_in = pair_moved(current, 1), pair_moved(field, -1)
        last = [far, *previous] if previous else []
        (early,) = call(early_body, [field_shape], [own, current] + last)
        received = [near, first, second, early]
        past = [history[0], other_history] if step < pairs else []
        previous = [first, second, current]
        if step < steps - 1:
            (field,) = call(
                functools.partial(late_body, step, pairs), [current_shape], received + [field_in] + past
            )
            current, going = call(
                functools.partial(next_body, step),
                [current_shape, current_shape],
                [diagonal_block_inverses, excitation, field, swapped(field), current_in],
            )
        else:
            if step < rounds - 1:
                windows = halo(current_in, True), halo(current_in, False)
            even, odd = call(
                last_body,
                [field_shape, field_shape],
                received + [far, own, current],
                after=collected,
                microseconds=0.5 if step < rounds - 1 else 20,
            )
            mine, send, field = call(
                functools.partial(share_body, step, steps, pairs),
                [field_shape, current_shape, current_shape],
                [even, odd, field_in] + past,
            )
            (result,) = call(
                functools.partial(finish_body, step, steps),
                [field_shape],
                [mine, swapped(send)] + ([result] if step >= steps else []),
            )
            current, going = current_in, field
    return (out, result[None])


def solution(mesh):
    placed = (
        P("delay", "surface", None, None, None),
        P("delay", "surface", None),
        P("surface", None, None),
        P(None, "surface", None),
        P("delay", "surface", None),
    )
    return jax.shard_map(
        per_device,
        mesh=mesh,
        in_specs=placed,
        out_specs=(P(None, "surface", None), P("delay", "surface", None)),
        check_vma=False,
    )
```

```python
import functools

import jax
import jax.numpy as jnp
from jax import lax
from jax.experimental import pallas as pl
from jax.experimental.pallas import tpu as pltpu
from jax.sharding import PartitionSpec as P

F32 = jnp.float32
BF16 = jnp.bfloat16
AXES = ("delay", "surface")
VMEM = pl.BlockSpec(memory_space=pltpu.VMEM)
MIB = 1024 * 1024
TOKEN = jax.ShapeDtypeStruct((8, 128), F32)


def dot(a, b):
    return jnp.dot(a, b, preferred_element_type=F32)


def place():
    lag = lax.axis_index("delay")
    return lax.rem(lag, 2), lax.div(lag, 2)


def cost(microseconds):
    moved = int(3.6e6 * microseconds)
    return pl.CostEstimate(flops=0, bytes_accessed=moved, transcendentals=0)


def call(body, outs, args, after=None, field_last=False, microseconds=0.5):
    specs = [VMEM] * len(args)
    if field_last:
        args = args[1:] + args[:1]
        body = functools.partial(field_to_front, body, len(args))
    if after is not None:
        args, specs = [after] + args, [pl.BlockSpec(memory_space=pl.ANY)] + specs
        body = functools.partial(skip_first, body)
    return pl.pallas_call(
        body,
        out_shape=tuple(outs),
        in_specs=specs,
        out_specs=tuple(VMEM for _ in outs),
        cost_estimate=cost(microseconds),
        compiler_params=pltpu.CompilerParams(vmem_limit_bytes=8 * MIB),
    )(*args)


def field_to_front(body, count, *refs):
    body(refs[count - 1], *refs[: count - 1], *refs[count:])


def skip_first(body, _, *refs):
    body(*refs)


def spread_body(groups, pattern_ref, entries_ref, keep_ref, own_ref, *rest):
    *send_refs, here_ref, all_ref, slots_ref, sems, slots_sem = rest
    core, _ = place()
    blocks, slots, size, _ = entries_ref.shape
    slots_copy = pltpu.make_async_copy(pattern_ref, slots_ref, slots_sem)
    slots_copy.start()
    copies = [
        pltpu.make_async_copy(entries_ref.at[row], here_ref.at[row], sems.at[row])
        for row in range(blocks)
    ]
    for copy in copies:
        copy.start()
    base = (lax.axis_index("surface") - 2) * blocks
    total = groups * blocks
    all_ref[...] = jnp.zeros_like(all_ref)
    slots_copy.wait()
    width = 2 * blocks * size
    mine = pl.ds(pl.multiple_of(core * width, width), width)
    other = pl.ds(pl.multiple_of((1 - core) * width, width), width)
    for row in range(blocks):
        copies[row].wait()
        rows = slice(row * size, (row + 1) * size)
        for slot in range(slots):
            j = lax.rem(slots_ref[row, slot] - base + total, total)
            column = jnp.where(
                j < 2 * blocks,
                jnp.where(j < blocks, j + blocks, j - blocks),
                jnp.where(j < 3 * blocks, j + 2 * blocks, j - blocks),
            )
            columns = pl.ds(pl.multiple_of(column * size, size), size)
            all_ref[rows, columns] = here_ref[row, slot]
        keep_ref[rows, :] = all_ref[rows, mine]
        own_ref[rows, :] = all_ref[rows, 2 * width :]
        send_refs[row][...] = all_ref[rows, other]


def spread(entries, pattern, groups):
    blocks, slots, size, _ = entries.shape
    side = blocks * size

    def matrix(rows, columns):
        return jax.ShapeDtypeStruct((rows, columns), entries.dtype)

    return pl.pallas_call(
        functools.partial(spread_body, groups),
        out_shape=(matrix(side, 2 * side), matrix(side, side), *[matrix(size, 2 * side)] * blocks),
        in_specs=[pl.BlockSpec(memory_space=pl.ANY)] * 2,
        out_specs=(VMEM,) * (blocks + 2),
        scratch_shapes=[
            pltpu.VMEM(entries.shape, entries.dtype),
            pltpu.VMEM((side, 5 * side), entries.dtype),
            pltpu.SMEM(pattern.shape, pattern.dtype),
            pltpu.SemaphoreType.DMA((blocks,)),
            pltpu.SemaphoreType.DMA,
        ],
        cost_estimate=cost(4),
        compiler_params=pltpu.CompilerParams(vmem_limit_bytes=51 * MIB),
    )(pattern, entries)


def arrange_body(kept_ref, *rest):
    *got_refs, near_ref, far_ref = rest
    core, _ = place()

    def put(got_to_ref, kept_to_ref):
        kept_to_ref[...] = kept_ref[...]
        for i, got_ref in enumerate(got_refs):
            size = got_ref.shape[0]
            got_to_ref[i * size : (i + 1) * size, :] = got_ref[...]

    @pl.when(core == 0)
    def _():
        put(far_ref, near_ref)

    @pl.when(core == 1)
    def _():
        put(near_ref, far_ref)


def window(matrix_ref, first_ref, second_ref):
    rows = first_ref.shape[0]
    return dot(matrix_ref[:, :rows], first_ref[...]) + dot(matrix_ref[:, rows:], second_ref[...])


def early_body(own_ref, now_ref, *rest):
    *last, out_ref = rest
    core, _ = place()
    if last:
        far_ref, first_ref, second_ref, before_ref = last
        local = jnp.where(core == 0, now_ref[...], before_ref[...])
        out_ref[...] = dot(own_ref[...], local) + window(far_ref, first_ref, second_ref)
    else:
        local = jnp.where(core == 0, now_ref[...], jnp.zeros_like(now_ref))
        out_ref[...] = dot(own_ref[...], local)


def came(step, pairs, field_ref, history):
    core, pair = place()
    value = jnp.where(pair == pairs - 1, 0.0, field_ref[...].astype(F32))
    if history:
        mine_ref, other_ref = history
        past = jnp.where(pair == step, other_ref[...], mine_ref[...])
        special = jnp.logical_or(pair == step, pair == step + 1)
        value = jnp.where(special, jnp.where(core == 0, past, 0.0), value)
    return value


def late_body(step, pairs, field_ref, near_ref, first_ref, second_ref, early_ref, *rest):
    *history, out_ref = rest
    total = early_ref[...] + window(near_ref, first_ref, second_ref)
    out_ref[...] = (total + came(step, pairs, field_ref, history)).astype(BF16)


def last_body(near_ref, first_ref, second_ref, early_ref, far_ref, own_ref, now_ref, even_ref, odd_ref):
    core, _ = place()
    even_ref[...] = early_ref[...] + window(near_ref, first_ref, second_ref)
    local = jnp.where(core == 1, now_ref[...], jnp.zeros_like(now_ref))
    odd_ref[...] = window(far_ref, first_ref, second_ref) + dot(own_ref[...], local)


def share_body(step, steps, pairs, even_ref, odd_ref, field_ref, *rest):
    *rest, keep_ref, send_ref = rest
    history, field_out_ref = (rest[:-1], rest[-1]) if step < steps + pairs - 2 else (rest, None)
    core, pair = place()
    even = even_ref[...] + came(step, pairs, field_ref, history)
    odd = odd_ref[...]
    ended = pair == step - steps
    late = field_ref[...].astype(F32)
    keep_ref[...] = jnp.where(ended, late, jnp.where(core == 1, odd, even))
    send_ref[...] = jnp.where(ended, late, jnp.where(core == 0, odd, even)).astype(BF16)
    if field_out_ref is not None:
        field_out_ref[...] = even.astype(BF16)


def finish_body(step, steps, mine_ref, other_ref, *rest):
    *earlier, result_ref = rest
    core, pair = place()
    field = mine_ref[...] + other_ref[...].astype(F32)
    if earlier:
        before = earlier[0][...]
        ended = pair == step - steps
        adds = jnp.logical_and(ended, core == 1)
        field = jnp.where(
            adds, before + field, jnp.where(pair == step - (steps - 1), field, before)
        )
    result_ref[...] = field


def collect_body(pairs, *refs):
    *seen, out_ref, token_ref = refs
    token_ref[...] = jnp.zeros_like(token_ref)
    _, pair = place()
    for step in range(out_ref.shape[0]):
        value = seen[step][...]
        for later in range(1, pairs):
            value = jnp.where(pair == later, seen[step + later][...], value)
        out_ref[step] = value


def solve(inverse_ref, rhs, out_ref, keep, other):
    size = inverse_ref.shape[1]
    fresh = []
    for i in range(inverse_ref.shape[0]):
        rows = slice(i * size, (i + 1) * size)
        block = dot(inverse_ref[i], rhs[rows]).astype(BF16)
        fresh.append(jnp.where(keep, block, other[rows]))
        out_ref[rows, :] = fresh[-1]
    return fresh


def first_history_body(history_ref, other_history_ref, out_ref):
    core, _ = place()
    out_ref[...] = jnp.where(core == 0, history_ref[...], other_history_ref[...])


def start_body(inverse_ref, excitation_ref, history_ref, out_ref):
    _, pair = place()
    rhs = (excitation_ref[0].astype(F32) - history_ref[...]).astype(BF16)
    solve(inverse_ref, rhs, out_ref, pair == 0, jnp.zeros_like(rhs))


def next_body(step, inverse_ref, excitation_ref, mine_ref, other_ref, came_ref, out_ref, going_ref):
    _, pair = place()
    field = mine_ref[...].astype(F32) + other_ref[...].astype(F32)
    rhs = (excitation_ref[step + 1].astype(F32) - field).astype(BF16)
    first_pair = pair == 0
    size = inverse_ref.shape[1]
    for i, block in enumerate(solve(inverse_ref, rhs, out_ref, first_pair, came_ref)):
        rows = slice(i * size, (i + 1) * size)
        going_ref[rows, :] = jnp.where(first_pair, block, mine_ref[rows, :])


def per_device(lagged_block_entries, pattern, diagonal_block_inverses, excitation, history):
    lags, groups = lax.axis_size("delay"), lax.axis_size("surface")
    pairs = lags // 2
    entries = lagged_block_entries[0]
    blocks, slots, size, _ = entries.shape
    steps, rows, columns = excitation.shape

    def device(d, s):
        return d * groups + s

    def everyone(move):
        return [
            (device(d, s), device(*move(d, s))) for d in range(lags) for s in range(groups)
        ]

    def swapped(value):
        return lax.ppermute(value, AXES, everyone(lambda d, s: (d ^ 1, s)))

    def pair_moved(value, hop):
        return lax.ppermute(value, AXES, everyone(lambda d, s: ((d + 2 * hop) % lags, s)))

    def halo(value, hop):
        return lax.ppermute(
            value, AXES, everyone(lambda d, s: (d, (s + (hop if d % 2 == 0 else -hop)) % groups))
        )

    other_history = swapped(history[0])
    field_shape = jax.ShapeDtypeStruct((rows, columns), F32)
    current_shape = jax.ShapeDtypeStruct((rows, columns), BF16)
    kept, own, *sent = spread(entries, pattern[0], groups)
    (first_history,) = call(first_history_body, [field_shape], [history[0], other_history])
    (current,) = call(
        start_body,
        [current_shape],
        [diagonal_block_inverses, excitation, first_history],
    )
    matrix_shape = jax.ShapeDtypeStruct((rows, 2 * rows), kept.dtype)
    near, far = call(arrange_body, [matrix_shape, matrix_shape], [kept] + [swapped(part) for part in sent])

    going = field = current
    seen = []
    previous = []
    result = []
    out = collected = None
    rounds = steps + pairs - 1
    windows = None
    for step in range(rounds):
        seen.append(current)
        if step == rounds - 1:
            out, collected = call(
                functools.partial(collect_body, pairs),
                [jax.ShapeDtypeStruct(excitation.shape, BF16), TOKEN],
                seen,
            )
        first, second = windows or (halo(current, 1), halo(current, 2))
        if pairs == 2:
            current_in = field_in = pair_moved(going, 1)
        else:
            current_in, field_in = pair_moved(current, 1), pair_moved(field, -1)
        last = [far, *previous] if previous else []
        (early,) = call(early_body, [field_shape], [own, current] + last)
        received = [near, first, second, early]
        past = [history[0], other_history] if step < pairs else []
        previous = [first, second, current]
        if step < steps - 1:
            (field,) = call(
                functools.partial(late_body, step, pairs),
                [current_shape],
                [field_in] + received + past,
                field_last=step != 1,
            )
            current, going = call(
                functools.partial(next_body, step),
                [current_shape, current_shape],
                [diagonal_block_inverses, excitation, field, swapped(field), current_in],
            )
        else:
            if step < rounds - 1:
                windows = halo(current_in, 1), halo(current_in, 2)
            even, odd = call(
                last_body,
                [field_shape, field_shape],
                received + [far, own, current],
                after=collected,
                microseconds=0.5 if step < rounds - 1 else 20,
            )
            *fields, mine, send = call(
                functools.partial(share_body, step, steps, pairs),
                [current_shape] * (step < rounds - 1) + [field_shape, current_shape],
                [even, odd, field_in] + past,
            )
            field = fields[0] if fields else None
            (result,) = call(
                functools.partial(finish_body, step, steps),
                [field_shape],
                [mine, swapped(send)] + ([result] if step >= steps else []),
            )
            current, going = current_in, field
    return (out, result[None])


def solution(mesh):
    placed = (
        P("delay", "surface", None, None, None),
        P("delay", "surface", None),
        P("surface", None, None),
        P(None, "surface", None),
        P("delay", "surface", None),
    )
    return jax.shard_map(
        per_device,
        mesh=mesh,
        in_specs=placed,
        out_specs=(P(None, "surface", None), P("delay", "surface", None)),
        check_vma=False,
    )
```

```python
import functools

import jax
import jax.numpy as jnp
from jax import lax
from jax.experimental import pallas as pl
from jax.experimental.pallas import tpu as pltpu
from jax.sharding import PartitionSpec as P

F32 = jnp.float32
BF16 = jnp.bfloat16
AXES = ("delay", "surface")
VMEM = pl.BlockSpec(memory_space=pltpu.VMEM)
MIB = 1024 * 1024
TOKEN = jax.ShapeDtypeStruct((8, 128), F32)


def dot(a, b):
    return jnp.dot(a, b, preferred_element_type=F32)


def place():
    lag = lax.axis_index("delay")
    return lax.rem(lag, 2), lax.div(lag, 2)


def cost(microseconds):
    moved = int(3.6e6 * microseconds)
    return pl.CostEstimate(flops=0, bytes_accessed=moved, transcendentals=0)


def call(body, outs, args, after=None, field_last=False, microseconds=0.5):
    specs = [VMEM] * len(args)
    if field_last:
        args = args[1:] + args[:1]
        body = functools.partial(field_to_front, body, len(args))
    if after is not None:
        args, specs = [after] + args, [pl.BlockSpec(memory_space=pl.ANY)] + specs
        body = functools.partial(skip_first, body)
    return pl.pallas_call(
        body,
        out_shape=tuple(outs),
        in_specs=specs,
        out_specs=tuple(VMEM for _ in outs),
        cost_estimate=cost(microseconds),
        compiler_params=pltpu.CompilerParams(vmem_limit_bytes=8 * MIB),
    )(*args)


def field_to_front(body, count, *refs):
    body(refs[count - 1], *refs[: count - 1], *refs[count:])


def skip_first(body, _, *refs):
    body(*refs)


def spread_body(groups, pattern_ref, entries_ref, keep_ref, own_ref, *rest):
    *send_refs, here_ref, all_ref, slots_ref, sems, slots_sem = rest
    core, _ = place()
    blocks, slots, size, _ = entries_ref.shape
    slots_copy = pltpu.make_async_copy(pattern_ref, slots_ref, slots_sem)
    slots_copy.start()
    copies = [
        pltpu.make_async_copy(entries_ref.at[row], here_ref.at[row], sems.at[row])
        for row in range(blocks)
    ]
    for copy in copies:
        copy.start()
    base = (lax.axis_index("surface") - 2) * blocks
    total = groups * blocks
    all_ref[...] = jnp.zeros_like(all_ref)
    slots_copy.wait()
    width = 2 * blocks * size
    mine = pl.ds(pl.multiple_of(core * width, width), width)
    other = pl.ds(pl.multiple_of((1 - core) * width, width), width)
    for row in range(blocks):
        copies[row].wait()
        rows = slice(row * size, (row + 1) * size)
        for slot in range(slots):
            j = lax.rem(slots_ref[row, slot] - base + total, total)
            column = jnp.where(
                j < 2 * blocks,
                jnp.where(j < blocks, j + blocks, j - blocks),
                jnp.where(j < 3 * blocks, j + 2 * blocks, j - blocks),
            )
            columns = pl.ds(pl.multiple_of(column * size, size), size)
            all_ref[rows, columns] = here_ref[row, slot]
        keep_ref[rows, :] = all_ref[rows, mine]
        own_ref[rows, :] = all_ref[rows, 2 * width :]
        send_refs[row][...] = all_ref[rows, other]


def spread(entries, pattern, groups):
    blocks, slots, size, _ = entries.shape
    side = blocks * size

    def matrix(rows, columns):
        return jax.ShapeDtypeStruct((rows, columns), entries.dtype)

    return pl.pallas_call(
        functools.partial(spread_body, groups),
        out_shape=(matrix(side, 2 * side), matrix(side, side), *[matrix(size, 2 * side)] * blocks),
        in_specs=[pl.BlockSpec(memory_space=pl.ANY)] * 2,
        out_specs=(VMEM,) * (blocks + 2),
        scratch_shapes=[
            pltpu.VMEM(entries.shape, entries.dtype),
            pltpu.VMEM((side, 5 * side), entries.dtype),
            pltpu.SMEM(pattern.shape, pattern.dtype),
            pltpu.SemaphoreType.DMA((blocks,)),
            pltpu.SemaphoreType.DMA,
        ],
        cost_estimate=cost(4),
        compiler_params=pltpu.CompilerParams(vmem_limit_bytes=51 * MIB),
    )(pattern, entries)


def arrange_body(kept_ref, *rest):
    *got_refs, near_ref, far_ref = rest
    core, _ = place()

    def put(got_to_ref, kept_to_ref):
        kept_to_ref[...] = kept_ref[...]
        for i, got_ref in enumerate(got_refs):
            size = got_ref.shape[0]
            got_to_ref[i * size : (i + 1) * size, :] = got_ref[...]

    @pl.when(core == 0)
    def _():
        put(far_ref, near_ref)

    @pl.when(core == 1)
    def _():
        put(near_ref, far_ref)


def window(matrix_ref, first_ref, second_ref):
    rows = first_ref.shape[0]
    return dot(matrix_ref[:, :rows], first_ref[...]) + dot(matrix_ref[:, rows:], second_ref[...])


def early_body(own_ref, now_ref, *rest):
    *last, out_ref = rest
    core, _ = place()
    if last:
        far_ref, first_ref, second_ref, before_ref = last
        local = jnp.where(core == 0, now_ref[...], before_ref[...])
        out_ref[...] = dot(own_ref[...], local) + window(far_ref, first_ref, second_ref)
    else:
        local = jnp.where(core == 0, now_ref[...], jnp.zeros_like(now_ref))
        out_ref[...] = dot(own_ref[...], local)


def came(step, pairs, field_ref, history):
    core, pair = place()
    value = jnp.where(pair == pairs - 1, 0.0, field_ref[...].astype(F32))
    if history:
        mine_ref, other_ref = history
        past = jnp.where(pair == step, other_ref[...], mine_ref[...])
        special = jnp.logical_or(pair == step, pair == step + 1)
        value = jnp.where(special, jnp.where(core == 0, past, 0.0), value)
    return value


def late_body(step, pairs, field_ref, near_ref, first_ref, second_ref, early_ref, *rest):
    *history, out_ref = rest
    total = early_ref[...] + window(near_ref, first_ref, second_ref)
    out_ref[...] = (total + came(step, pairs, field_ref, history)).astype(BF16)


def even_body(step, pairs, near_ref, first_ref, second_ref, early_ref, *rest):
    *field, even_ref, out_ref = rest
    total = early_ref[...] + window(near_ref, first_ref, second_ref)
    if field:
        total += came(step, pairs, field[0], field[1:])
    even_ref[...] = total
    out_ref[...] = total.astype(BF16)


def odd_body(even_ref, far_ref, first_ref, second_ref, own_ref, now_ref, keep_ref, send_ref):
    core, _ = place()
    local = jnp.where(core == 1, now_ref[...], jnp.zeros_like(now_ref))
    odd = window(far_ref, first_ref, second_ref) + dot(own_ref[...], local)
    even = even_ref[...]
    keep_ref[...] = jnp.where(core == 1, odd, even)
    send_ref[...] = jnp.where(core == 0, odd, even).astype(BF16)


def finish_body(step, steps, *refs):
    *earlier, mine_ref, other_ref, result_ref = refs
    core, pair = place()
    field = mine_ref[...] + other_ref[...].astype(F32)
    if earlier:
        before_ref, straight_ref, crossed_ref = earlier
        adds = jnp.logical_and(core == 1, pair == step - steps)
        rest = straight_ref[...].astype(F32) + crossed_ref[...].astype(F32)
        before = before_ref[...] + jnp.where(adds, rest, 0.0)
        field = jnp.where(pair == step - (steps - 1), field, before)
    result_ref[...] = field


def collect_body(pairs, *refs):
    *seen, out_ref, token_ref = refs
    token_ref[...] = jnp.zeros_like(token_ref)
    _, pair = place()
    for step in range(out_ref.shape[0]):
        value = seen[step][...]
        for later in range(1, pairs):
            value = jnp.where(pair == later, seen[step + later][...], value)
        out_ref[step] = value


def solve(inverse_ref, rhs, out_ref, keep, other):
    size = inverse_ref.shape[1]
    fresh = []
    for i in range(inverse_ref.shape[0]):
        rows = slice(i * size, (i + 1) * size)
        block = dot(inverse_ref[i], rhs[rows]).astype(BF16)
        fresh.append(jnp.where(keep, block, other[rows]))
        out_ref[rows, :] = fresh[-1]
    return fresh


def first_history_body(history_ref, other_history_ref, out_ref):
    core, _ = place()
    out_ref[...] = jnp.where(core == 0, history_ref[...], other_history_ref[...])


def start_body(inverse_ref, excitation_ref, history_ref, out_ref):
    _, pair = place()
    rhs = (excitation_ref[0].astype(F32) - history_ref[...]).astype(BF16)
    solve(inverse_ref, rhs, out_ref, pair == 0, jnp.zeros_like(rhs))


def next_body(step, inverse_ref, excitation_ref, mine_ref, other_ref, came_ref, out_ref, going_ref):
    _, pair = place()
    field = mine_ref[...].astype(F32) + other_ref[...].astype(F32)
    rhs = (excitation_ref[step + 1].astype(F32) - field).astype(BF16)
    first_pair = pair == 0
    size = inverse_ref.shape[1]
    for i, block in enumerate(solve(inverse_ref, rhs, out_ref, first_pair, came_ref)):
        rows = slice(i * size, (i + 1) * size)
        going_ref[rows, :] = jnp.where(first_pair, block, mine_ref[rows, :])


def per_device(lagged_block_entries, pattern, diagonal_block_inverses, excitation, history):
    lags, groups = lax.axis_size("delay"), lax.axis_size("surface")
    pairs = lags // 2
    entries = lagged_block_entries[0]
    blocks, slots, size, _ = entries.shape
    steps, rows, columns = excitation.shape

    def device(d, s):
        return d * groups + s

    def everyone(move):
        return [
            (device(d, s), device(*move(d, s))) for d in range(lags) for s in range(groups)
        ]

    def swapped(value):
        return lax.ppermute(value, AXES, everyone(lambda d, s: (d ^ 1, s)))

    def pair_moved(value, hop):
        return lax.ppermute(value, AXES, everyone(lambda d, s: ((d + 2 * hop) % lags, s)))

    def crossed(value):
        return lax.ppermute(value, AXES, everyone(lambda d, s: (((d - 2) % lags) ^ 1, s)))

    def halo(value, hop):
        return lax.ppermute(
            value, AXES, everyone(lambda d, s: (d, (s + (hop if d % 2 == 0 else -hop)) % groups))
        )

    other_history = swapped(history[0])
    field_shape = jax.ShapeDtypeStruct((rows, columns), F32)
    current_shape = jax.ShapeDtypeStruct((rows, columns), BF16)
    kept, own, *sent = spread(entries, pattern[0], groups)
    (first_history,) = call(first_history_body, [field_shape], [history[0], other_history])
    (current,) = call(
        start_body,
        [current_shape],
        [diagonal_block_inverses, excitation, first_history],
    )
    matrix_shape = jax.ShapeDtypeStruct((rows, 2 * rows), kept.dtype)
    near, far = call(arrange_body, [matrix_shape, matrix_shape], [kept] + [swapped(part) for part in sent])

    going = field = current
    seen = []
    previous = []
    result = []
    out = collected = None
    rounds = steps + pairs - 1
    windows = None
    for step in range(rounds):
        seen.append(current)
        if step == rounds - 1:
            out, collected = call(
                functools.partial(collect_body, pairs),
                [jax.ShapeDtypeStruct(excitation.shape, BF16), TOKEN],
                seen,
            )
        first, second = windows or (halo(current, 1), halo(current, 2))
        if pairs == 2:
            current_in = field_in = pair_moved(going, 1)
        else:
            current_in, field_in = pair_moved(current, 1), pair_moved(field, -1)
        last = [far, *previous] if previous else []
        (early,) = call(early_body, [field_shape], [own, current] + last)
        received = [near, first, second, early]
        past = [history[0], other_history] if step < pairs else []
        previous = [first, second, current]
        if step < steps - 1:
            (field,) = call(
                functools.partial(late_body, step, pairs),
                [current_shape],
                [field_in] + received + past,
                field_last=step != 1,
            )
            current, going = call(
                functools.partial(next_body, step),
                [current_shape, current_shape],
                [diagonal_block_inverses, excitation, field, swapped(field), current_in],
            )
        else:
            if step < rounds - 1:
                windows = halo(current_in, 1), halo(current_in, 2)
            even, next_field = call(
                functools.partial(even_body, step, pairs),
                [field_shape, current_shape],
                received + ([field_in] + past if step < rounds - 1 else []),
            )
            mine, send = call(
                odd_body,
                [field_shape, current_shape],
                [even, far, first, second, own, current],
                after=collected,
            )
            earlier = [result, field_in, crossed(field)] if step >= steps else []
            (result,) = call(
                functools.partial(finish_body, step, steps),
                [field_shape],
                earlier + [mine, swapped(send)],
            )
            field = next_field
            current, going = current_in, field
    return (out, result[None])


def solution(mesh):
    placed = (
        P("delay", "surface", None, None, None),
        P("delay", "surface", None),
        P("surface", None, None),
        P(None, "surface", None),
        P("delay", "surface", None),
    )
    return jax.shard_map(
        per_device,
        mesh=mesh,
        in_specs=placed,
        out_specs=(P(None, "surface", None), P("delay", "surface", None)),
        check_vma=False,
    )
```

```python
import functools

import jax
import jax.numpy as jnp
from jax import lax
from jax.experimental import pallas as pl
from jax.experimental.pallas import tpu as pltpu
from jax.sharding import PartitionSpec as P

F32 = jnp.float32
BF16 = jnp.bfloat16
AXES = ("delay", "surface")
VMEM = pl.BlockSpec(memory_space=pltpu.VMEM)
MIB = 1024 * 1024
TOKEN = jax.ShapeDtypeStruct((8, 128), F32)


def dot(a, b):
    return jnp.dot(a, b, preferred_element_type=F32)


def place():
    lag = lax.axis_index("delay")
    return lax.rem(lag, 2), lax.div(lag, 2)


COST = pl.CostEstimate(flops=0, bytes_accessed=1 << 20, transcendentals=0)


def call(body, outs, args, after=None, in_front=None):
    specs = [VMEM] * len(args)
    if in_front is not None:
        args = args[in_front : in_front + 1] + args[:in_front] + args[in_front + 1 :]
        body = functools.partial(put_back, body, in_front)
    if after is not None:
        body = functools.partial(skip, body, len(args))
        args, specs = args + [after], specs + [pl.BlockSpec(memory_space=pl.ANY)]
    return pl.pallas_call(
        body,
        out_shape=tuple(outs),
        in_specs=specs,
        out_specs=tuple(VMEM for _ in outs),
        cost_estimate=COST,
        compiler_params=pltpu.CompilerParams(vmem_limit_bytes=8 * MIB),
    )(*args)


def put_back(body, in_front, moved, *refs):
    body(*refs[:in_front], moved, *refs[in_front:])


def skip(body, number, *refs):
    body(*refs[:number], *refs[number + 1 :])


def spread_body(groups, pattern_ref, entries_ref, keep_ref, own_ref, *rest):
    *send_refs, here_ref, all_ref, slots_ref, sems, slots_sem = rest
    core, _ = place()
    blocks, slots, size, _ = entries_ref.shape
    slots_copy = pltpu.make_async_copy(pattern_ref, slots_ref, slots_sem)
    slots_copy.start()
    copies = [
        pltpu.make_async_copy(entries_ref.at[row], here_ref.at[row], sems.at[row])
        for row in range(blocks)
    ]
    for copy in copies:
        copy.start()
    base = (lax.axis_index("surface") - 2) * blocks
    total = groups * blocks
    all_ref[...] = jnp.zeros_like(all_ref)
    slots_copy.wait()
    width = 2 * blocks * size
    mine = pl.ds(pl.multiple_of(core * width, width), width)
    other = pl.ds(pl.multiple_of((1 - core) * width, width), width)
    for row in range(blocks):
        copies[row].wait()
        rows = slice(row * size, (row + 1) * size)
        for slot in range(slots):
            j = lax.rem(slots_ref[row, slot] - base + total, total)
            column = jnp.where(
                j < 2 * blocks,
                jnp.where(j < blocks, j + blocks, j - blocks),
                jnp.where(j < 3 * blocks, j + 2 * blocks, j - blocks),
            )
            columns = pl.ds(pl.multiple_of(column * size, size), size)
            all_ref[rows, columns] = here_ref[row, slot]
        keep_ref[rows, :] = all_ref[rows, mine]
        own_ref[rows, :] = all_ref[rows, 2 * width :]
        send_refs[row][...] = all_ref[rows, other]


def spread(entries, pattern, groups):
    blocks, slots, size, _ = entries.shape
    side = blocks * size

    def matrix(rows, columns):
        return jax.ShapeDtypeStruct((rows, columns), entries.dtype)

    return pl.pallas_call(
        functools.partial(spread_body, groups),
        out_shape=(matrix(side, 2 * side), matrix(side, side), *[matrix(size, 2 * side)] * blocks),
        in_specs=[pl.BlockSpec(memory_space=pl.ANY)] * 2,
        out_specs=(VMEM,) * (blocks + 2),
        scratch_shapes=[
            pltpu.VMEM(entries.shape, entries.dtype),
            pltpu.VMEM((side, 5 * side), entries.dtype),
            pltpu.SMEM(pattern.shape, pattern.dtype),
            pltpu.SemaphoreType.DMA((blocks,)),
            pltpu.SemaphoreType.DMA,
        ],
        cost_estimate=COST,
        compiler_params=pltpu.CompilerParams(vmem_limit_bytes=51 * MIB),
    )(pattern, entries)


def arrange_body(kept_ref, *rest):
    *got_refs, near_ref, far_ref = rest
    core, _ = place()

    def put(got_to_ref, kept_to_ref):
        kept_to_ref[...] = kept_ref[...]
        for i, got_ref in enumerate(got_refs):
            size = got_ref.shape[0]
            got_to_ref[i * size : (i + 1) * size, :] = got_ref[...]

    @pl.when(core == 0)
    def _():
        put(far_ref, near_ref)

    @pl.when(core == 1)
    def _():
        put(near_ref, far_ref)


def half(matrix_ref, block_ref, which):
    rows = block_ref.shape[0]
    return dot(matrix_ref[:, which * rows : (which + 1) * rows], block_ref[...])


def window(matrix_ref, first_ref, second_ref):
    return half(matrix_ref, first_ref, 0) + half(matrix_ref, second_ref, 1)


def early_body(own_ref, now_ref, *rest):
    *last, out_ref = rest
    core, _ = place()
    if last:
        far_ref, first_ref, second_ref, before_ref = last
        local = jnp.where(core == 0, now_ref[...], before_ref[...])
        out_ref[...] = dot(own_ref[...], local) + window(far_ref, first_ref, second_ref)
    else:
        local = jnp.where(core == 0, now_ref[...], jnp.zeros_like(now_ref))
        out_ref[...] = dot(own_ref[...], local)


def came(step, pairs, field_ref, history):
    core, pair = place()
    value = jnp.where(pair == pairs - 1, 0.0, field_ref[...].astype(F32))
    if history:
        mine_ref, other_ref = history
        past = jnp.where(pair == step, other_ref[...], mine_ref[...])
        special = jnp.logical_or(pair == step, pair == step + 1)
        value = jnp.where(special, jnp.where(core == 0, past, 0.0), value)
    return value


def first_body(near_ref, first_ref, early_ref, out_ref):
    out_ref[...] = early_ref[...] + half(near_ref, first_ref, 0)


def late_body(step, pairs, near_ref, second_ref, early_ref, field_ref, *rest):
    *history, out_ref = rest
    total = early_ref[...] + half(near_ref, second_ref, 1)
    out_ref[...] = (total + came(step, pairs, field_ref, history)).astype(BF16)


def even_body(step, pairs, near_ref, second_ref, early_ref, *rest):
    total = early_ref[...] + half(near_ref, second_ref, 1)
    if len(rest) == 1:
        rest[0][...] = total
        return
    field_ref, *history, even_ref, out_ref = rest
    total += came(step, pairs, field_ref, history)
    even_ref[...] = total
    out_ref[...] = total.astype(BF16)


def odd_early_body(own_ref, now_ref, out_ref):
    core, _ = place()
    out_ref[...] = dot(own_ref[...], jnp.where(core == 1, now_ref[...], jnp.zeros_like(now_ref)))


def odd_body(which, far_ref, block_ref, early_ref, out_ref):
    out_ref[...] = early_ref[...] + half(far_ref, block_ref, which)


def share_body(step, steps, even_ref, odd_ref, *rest):
    *field, keep_ref, send_ref = rest
    core, pair = place()
    even, odd = even_ref[...], odd_ref[...]
    if field:
        ended = pair == step - steps
        came_late = field[0][...].astype(F32)
        even, odd = jnp.where(ended, came_late, even), jnp.where(ended, came_late, odd)
    keep_ref[...] = jnp.where(core == 1, odd, even)
    send_ref[...] = jnp.where(core == 0, odd, even).astype(BF16)


def finish_body(step, steps, mine_ref, other_ref, *rest):
    *earlier, result_ref = rest
    core, pair = place()
    field = mine_ref[...] + other_ref[...].astype(F32)
    if earlier:
        before = earlier[0][...]
        adds = jnp.logical_and(core == 1, pair == step - steps)
        field = jnp.where(
            adds, before + field, jnp.where(pair == step - (steps - 1), field, before)
        )
    result_ref[...] = field


def collect_body(pairs, *refs):
    *seen, out_ref, token_ref = refs
    token_ref[...] = jnp.zeros_like(token_ref)
    _, pair = place()
    for step in range(out_ref.shape[0]):
        value = seen[step][...]
        for later in range(1, pairs):
            value = jnp.where(pair == later, seen[step + later][...], value)
        out_ref[step] = value


def solve(inverse_ref, rhs, out_ref, keep, other):
    size = inverse_ref.shape[1]
    fresh = []
    for i in range(inverse_ref.shape[0]):
        rows = slice(i * size, (i + 1) * size)
        block = dot(inverse_ref[i], rhs[rows]).astype(BF16)
        fresh.append(jnp.where(keep, block, other[rows]))
        out_ref[rows, :] = fresh[-1]
    return fresh


def first_history_body(history_ref, other_history_ref, out_ref):
    core, _ = place()
    out_ref[...] = jnp.where(core == 0, history_ref[...], other_history_ref[...])


def start_body(inverse_ref, excitation_ref, history_ref, out_ref):
    _, pair = place()
    rhs = (excitation_ref[0].astype(F32) - history_ref[...]).astype(BF16)
    solve(inverse_ref, rhs, out_ref, pair == 0, jnp.zeros_like(rhs))


def next_body(step, inverse_ref, excitation_ref, mine_ref, other_ref, came_ref, out_ref, going_ref):
    _, pair = place()
    field = mine_ref[...].astype(F32) + other_ref[...].astype(F32)
    rhs = (excitation_ref[step + 1].astype(F32) - field).astype(BF16)
    first_pair = pair == 0
    size = inverse_ref.shape[1]
    for i, block in enumerate(solve(inverse_ref, rhs, out_ref, first_pair, came_ref)):
        rows = slice(i * size, (i + 1) * size)
        going_ref[rows, :] = jnp.where(first_pair, block, mine_ref[rows, :])


def per_device(lagged_block_entries, pattern, diagonal_block_inverses, excitation, history):
    lags, groups = lax.axis_size("delay"), lax.axis_size("surface")
    pairs = lags // 2
    entries = lagged_block_entries[0]
    blocks, slots, size, _ = entries.shape
    steps, rows, columns = excitation.shape

    def device(d, s):
        return d * groups + s

    def everyone(move):
        return [
            (device(d, s), device(*move(d, s))) for d in range(lags) for s in range(groups)
        ]

    def swapped(value):
        return lax.ppermute(value, AXES, everyone(lambda d, s: (d ^ 1, s)))

    def pair_moved(value, hop):
        return lax.ppermute(value, AXES, everyone(lambda d, s: ((d + 2 * hop) % lags, s)))

    def halo(value, hop):
        return lax.ppermute(
            value, AXES, everyone(lambda d, s: (d, (s + (hop if d % 2 == 0 else -hop)) % groups))
        )

    other_history = swapped(history[0])
    field_shape = jax.ShapeDtypeStruct((rows, columns), F32)
    current_shape = jax.ShapeDtypeStruct((rows, columns), BF16)
    kept, own, *sent = spread(entries, pattern[0], groups)
    (first_history,) = call(first_history_body, [field_shape], [history[0], other_history])
    (current,) = call(
        start_body,
        [current_shape],
        [diagonal_block_inverses, excitation, first_history],
    )
    matrix_shape = jax.ShapeDtypeStruct((rows, 2 * rows), kept.dtype)
    near, far = call(arrange_body, [matrix_shape, matrix_shape], [kept] + [swapped(part) for part in sent])

    going = field = current
    seen = []
    previous = []
    result = None
    out = collected = None
    rounds = steps + pairs - 1
    windows = None
    for step in range(rounds):
        seen.append(current)
        if step == rounds - 1:
            out, collected = call(
                functools.partial(collect_body, pairs),
                [jax.ShapeDtypeStruct(excitation.shape, BF16), TOKEN],
                seen,
            )
        first, second = windows or (halo(current, 1), halo(current, 2))
        if pairs == 2:
            current_in = field_in = pair_moved(going, 1)
        else:
            current_in, field_in = pair_moved(current, 1), pair_moved(field, -1)
        last = [far, *previous] if previous else []
        (early,) = call(early_body, [field_shape], [own, current] + last)
        (partly,) = call(first_body, [field_shape], [near, first, early])
        received = [near, second, partly]
        past = [history[0], other_history] if step < pairs else []
        previous = [first, second, current]
        if step < steps - 1:
            (field,) = call(
                functools.partial(late_body, step, pairs),
                [current_shape],
                received + [field_in] + past,
                in_front=len(received) if step == 1 else None,
            )
            current, going = call(
                functools.partial(next_body, step),
                [current_shape, current_shape],
                [diagonal_block_inverses, excitation, field, swapped(field), current_in],
            )
        else:
            if step < rounds - 1:
                windows = halo(current_in, 1), halo(current_in, 2)
            more = step < rounds - 1
            even, *next_field = call(
                functools.partial(even_body, step, pairs),
                [field_shape] + [current_shape] * more,
                received + ([field_in] + past) * more,
            )
            (odd_early,) = call(odd_early_body, [field_shape], [own, current])
            for which, block in enumerate((first, second)):
                (odd_early,) = call(
                    functools.partial(odd_body, which), [field_shape], [far, block, odd_early]
                )
            mine, send = call(
                functools.partial(share_body, step, steps),
                [field_shape, current_shape],
                [even, odd_early] + [field_in] * (step >= steps),
            )
            (result,) = call(
                functools.partial(finish_body, step, steps),
                [field_shape],
                [mine, swapped(send)] + [result] * (step >= steps),
                after=collected,
            )
            field = next_field[0] if more else None
            current, going = current_in, field
    return (out, result[None])


def solution(mesh):
    placed = (
        P("delay", "surface", None, None, None),
        P("delay", "surface", None),
        P("surface", None, None),
        P(None, "surface", None),
        P("delay", "surface", None),
    )
    return jax.shard_map(
        per_device,
        mesh=mesh,
        in_specs=placed,
        out_specs=(P(None, "surface", None), P("delay", "surface", None)),
        check_vma=False,
    )
```

```python
import functools

import jax
import jax.numpy as jnp
from jax import lax
from jax.experimental import pallas as pl
from jax.experimental.pallas import tpu as pltpu
from jax.sharding import PartitionSpec as P

F32 = jnp.float32
BF16 = jnp.bfloat16
AXES = ("delay", "surface")
VMEM = pl.BlockSpec(memory_space=pltpu.VMEM)
MIB = 1024 * 1024
TOKEN = jax.ShapeDtypeStruct((8, 128), F32)


def dot(a, b):
    return jnp.dot(a, b, preferred_element_type=F32)


def place():
    lag = lax.axis_index("delay")
    return lax.rem(lag, 2), lax.div(lag, 2)


COST = pl.CostEstimate(flops=0, bytes_accessed=1 << 20, transcendentals=0)


def call(body, outs, args, after=None, in_front=None):
    specs = [VMEM] * len(args)
    if in_front is not None:
        args = args[in_front : in_front + 1] + args[:in_front] + args[in_front + 1 :]
        body = functools.partial(put_back, body, in_front)
    if after is not None:
        body = functools.partial(skip, body, len(args))
        args, specs = args + [after], specs + [pl.BlockSpec(memory_space=pl.ANY)]
    return pl.pallas_call(
        body,
        out_shape=tuple(outs),
        in_specs=specs,
        out_specs=tuple(VMEM for _ in outs),
        cost_estimate=COST,
        compiler_params=pltpu.CompilerParams(vmem_limit_bytes=8 * MIB),
    )(*args)


def put_back(body, in_front, moved, *refs):
    body(*refs[:in_front], moved, *refs[in_front:])


def skip(body, number, *refs):
    body(*refs[:number], *refs[number + 1 :])


def spread_body(groups, pattern_ref, entries_ref, keep_ref, own_ref, *rest):
    *send_refs, here_ref, all_ref, slots_ref, sems, slots_sem = rest
    core, _ = place()
    blocks, slots, size, _ = entries_ref.shape
    slots_copy = pltpu.make_async_copy(pattern_ref, slots_ref, slots_sem)
    slots_copy.start()
    copies = [
        pltpu.make_async_copy(entries_ref.at[row], here_ref.at[row], sems.at[row])
        for row in range(blocks)
    ]
    for copy in copies:
        copy.start()
    base = (lax.axis_index("surface") - 2) * blocks
    total = groups * blocks
    all_ref[...] = jnp.zeros_like(all_ref)
    slots_copy.wait()
    width = 2 * blocks * size
    mine = pl.ds(pl.multiple_of(core * width, width), width)
    other = pl.ds(pl.multiple_of((1 - core) * width, width), width)
    for row in range(blocks):
        copies[row].wait()
        rows = slice(row * size, (row + 1) * size)
        for slot in range(slots):
            j = lax.rem(slots_ref[row, slot] - base + total, total)
            column = jnp.where(
                j < 2 * blocks,
                jnp.where(j < blocks, j + blocks, j - blocks),
                jnp.where(j < 3 * blocks, j + 2 * blocks, j - blocks),
            )
            columns = pl.ds(pl.multiple_of(column * size, size), size)
            all_ref[rows, columns] = here_ref[row, slot]
        keep_ref[rows, :] = all_ref[rows, mine]
        own_ref[rows, :] = all_ref[rows, 2 * width :]
        send_refs[row][...] = all_ref[rows, other]


def spread(entries, pattern, groups):
    blocks, slots, size, _ = entries.shape
    side = blocks * size

    def matrix(rows, columns):
        return jax.ShapeDtypeStruct((rows, columns), entries.dtype)

    return pl.pallas_call(
        functools.partial(spread_body, groups),
        out_shape=(matrix(side, 2 * side), matrix(side, side), *[matrix(size, 2 * side)] * blocks),
        in_specs=[pl.BlockSpec(memory_space=pl.ANY)] * 2,
        out_specs=(VMEM,) * (blocks + 2),
        scratch_shapes=[
            pltpu.VMEM(entries.shape, entries.dtype),
            pltpu.VMEM((side, 5 * side), entries.dtype),
            pltpu.SMEM(pattern.shape, pattern.dtype),
            pltpu.SemaphoreType.DMA((blocks,)),
            pltpu.SemaphoreType.DMA,
        ],
        cost_estimate=COST,
        compiler_params=pltpu.CompilerParams(vmem_limit_bytes=51 * MIB),
    )(pattern, entries)


def arrange_body(kept_ref, *rest):
    *got_refs, near_ref, far_ref = rest
    core, _ = place()

    def put(got_to_ref, kept_to_ref):
        kept_to_ref[...] = kept_ref[...]
        for i, got_ref in enumerate(got_refs):
            size = got_ref.shape[0]
            got_to_ref[i * size : (i + 1) * size, :] = got_ref[...]

    @pl.when(core == 0)
    def _():
        put(far_ref, near_ref)

    @pl.when(core == 1)
    def _():
        put(near_ref, far_ref)


def half(matrix_ref, block_ref, which):
    rows = block_ref.shape[0]
    return dot(matrix_ref[:, which * rows : (which + 1) * rows], block_ref[...])


def window(matrix_ref, first_ref, second_ref):
    return half(matrix_ref, first_ref, 0) + half(matrix_ref, second_ref, 1)


def early_body(own_ref, now_ref, *rest):
    *last, out_ref = rest
    core, _ = place()
    if last:
        far_ref, first_ref, second_ref, before_ref = last
        local = jnp.where(core == 0, now_ref[...], before_ref[...])
        out_ref[...] = dot(own_ref[...], local) + window(far_ref, first_ref, second_ref)
    else:
        local = jnp.where(core == 0, now_ref[...], jnp.zeros_like(now_ref))
        out_ref[...] = dot(own_ref[...], local)


def came(step, pairs, field_ref, history):
    core, pair = place()
    value = jnp.where(pair == pairs - 1, 0.0, field_ref[...].astype(F32))
    if history:
        mine_ref, other_ref = history
        past = jnp.where(pair == step, other_ref[...], mine_ref[...])
        special = jnp.logical_or(pair == step, pair == step + 1)
        value = jnp.where(special, jnp.where(core == 0, past, 0.0), value)
    return value


def first_body(near_ref, first_ref, early_ref, out_ref):
    out_ref[...] = early_ref[...] + half(near_ref, first_ref, 0)


def late_body(step, pairs, near_ref, second_ref, early_ref, field_ref, *rest):
    *history, out_ref = rest
    total = early_ref[...] + half(near_ref, second_ref, 1)
    out_ref[...] = (total + came(step, pairs, field_ref, history)).astype(BF16)


def even_body(step, pairs, near_ref, second_ref, early_ref, *rest):
    total = early_ref[...] + half(near_ref, second_ref, 1)
    if len(rest) == 1:
        rest[0][...] = total
        return
    field_ref, *history, even_ref, out_ref = rest
    total += came(step, pairs, field_ref, history)
    even_ref[...] = total
    out_ref[...] = total.astype(BF16)


def odd_early_body(own_ref, now_ref, out_ref):
    core, _ = place()
    out_ref[...] = dot(own_ref[...], jnp.where(core == 1, now_ref[...], jnp.zeros_like(now_ref)))


def odd_body(which, far_ref, block_ref, early_ref, out_ref):
    out_ref[...] = early_ref[...] + half(far_ref, block_ref, which)


def share_body(step, steps, even_ref, odd_ref, *rest):
    *field, keep_ref, send_ref = rest
    core, pair = place()
    even, odd = even_ref[...], odd_ref[...]
    if field:
        ended = pair == step - steps
        came_late = field[0][...].astype(F32)
        even, odd = jnp.where(ended, came_late, even), jnp.where(ended, came_late, odd)
    keep_ref[...] = jnp.where(core == 1, odd, even)
    send_ref[...] = jnp.where(core == 0, odd, even).astype(BF16)


def finish_body(step, steps, mine_ref, other_ref, *rest):
    *earlier, result_ref = rest
    core, pair = place()
    field = mine_ref[...] + other_ref[...].astype(F32)
    if earlier:
        before = earlier[0][...]
        adds = jnp.logical_and(core == 1, pair == step - steps)
        field = jnp.where(
            adds, before + field, jnp.where(pair == step - (steps - 1), field, before)
        )
    result_ref[...] = field


def collect_body(pairs, *refs):
    *seen, out_ref, token_ref = refs
    token_ref[...] = jnp.zeros_like(token_ref)
    _, pair = place()
    for step in range(out_ref.shape[0]):
        value = seen[step][...]
        for later in range(1, pairs):
            value = jnp.where(pair == later, seen[step + later][...], value)
        out_ref[step] = value


def solve(inverse_ref, rhs, out_ref, keep, other):
    size = inverse_ref.shape[1]
    fresh = []
    for i in range(inverse_ref.shape[0]):
        rows = slice(i * size, (i + 1) * size)
        block = dot(inverse_ref[i], rhs[rows]).astype(BF16)
        fresh.append(jnp.where(keep, block, other[rows]))
        out_ref[rows, :] = fresh[-1]
    return fresh


def first_history_body(history_ref, other_history_ref, out_ref):
    core, _ = place()
    out_ref[...] = jnp.where(core == 0, history_ref[...], other_history_ref[...])


def start_body(inverse_ref, excitation_ref, history_ref, out_ref):
    _, pair = place()
    rhs = (excitation_ref[0].astype(F32) - history_ref[...]).astype(BF16)
    solve(inverse_ref, rhs, out_ref, pair == 0, jnp.zeros_like(rhs))


def next_body(step, inverse_ref, excitation_ref, mine_ref, other_ref, came_ref, out_ref, going_ref):
    _, pair = place()
    field = mine_ref[...].astype(F32) + other_ref[...].astype(F32)
    rhs = (excitation_ref[step + 1].astype(F32) - field).astype(BF16)
    first_pair = pair == 0
    size = inverse_ref.shape[1]
    for i, block in enumerate(solve(inverse_ref, rhs, out_ref, first_pair, came_ref)):
        rows = slice(i * size, (i + 1) * size)
        going_ref[rows, :] = jnp.where(first_pair, block, mine_ref[rows, :])


def per_device(lagged_block_entries, pattern, diagonal_block_inverses, excitation, history):
    lags, groups = lax.axis_size("delay"), lax.axis_size("surface")
    pairs = lags // 2
    entries = lagged_block_entries[0]
    blocks, slots, size, _ = entries.shape
    steps, rows, columns = excitation.shape

    def device(d, s):
        return d * groups + s

    def everyone(move):
        return [
            (device(d, s), device(*move(d, s))) for d in range(lags) for s in range(groups)
        ]

    def swapped(value):
        return lax.ppermute(value, AXES, everyone(lambda d, s: (d ^ 1, s)))

    def pair_moved(value, hop):
        return lax.ppermute(value, AXES, everyone(lambda d, s: ((d + 2 * hop) % lags, s)))

    def halo(value, hop, since=0, until=pairs):
        def move(d, s):
            if not since <= d // 2 <= until:
                return d ^ 1, s
            return d, (s + (hop if d % 2 == 0 else -hop)) % groups

        return lax.ppermute(value, AXES, everyone(move))

    other_history = swapped(history[0])
    field_shape = jax.ShapeDtypeStruct((rows, columns), F32)
    current_shape = jax.ShapeDtypeStruct((rows, columns), BF16)
    kept, own, *sent = spread(entries, pattern[0], groups)
    (first_history,) = call(first_history_body, [field_shape], [history[0], other_history])
    (current,) = call(
        start_body,
        [current_shape],
        [diagonal_block_inverses, excitation, first_history],
    )
    matrix_shape = jax.ShapeDtypeStruct((rows, 2 * rows), kept.dtype)
    near, far = call(arrange_body, [matrix_shape, matrix_shape], [kept] + [swapped(part) for part in sent])

    going = field = current
    seen = []
    previous = []
    result = None
    out = collected = None
    rounds = steps + pairs - 1
    windows = None
    for step in range(rounds):
        seen.append(current)
        if step == rounds - 1:
            out, collected = call(
                functools.partial(collect_body, pairs),
                [jax.ShapeDtypeStruct(excitation.shape, BF16), TOKEN],
                seen,
            )
        first, second = windows or (halo(current, 1, 0, step), halo(current, 2, 0, step))
        if pairs == 2:
            current_in = field_in = pair_moved(going, 1)
        else:
            current_in, field_in = pair_moved(current, 1), pair_moved(field, -1)
        last = [far, *previous] if previous else []
        (early,) = call(early_body, [field_shape], [own, current] + last)
        (partly,) = call(first_body, [field_shape], [near, first, early])
        received = [near, second, partly]
        past = [history[0], other_history] if step < pairs else []
        previous = [first, second, current]
        if step < steps - 1:
            (field,) = call(
                functools.partial(late_body, step, pairs),
                [current_shape],
                received + [field_in] + past,
                in_front=len(received) if step == 1 else None,
            )
            current, going = call(
                functools.partial(next_body, step),
                [current_shape, current_shape],
                [diagonal_block_inverses, excitation, field, swapped(field), current_in],
            )
        else:
            if step < rounds - 1:
                done = step + 2 - steps
                windows = halo(current_in, 1, done), halo(current_in, 2, done)
            more = step < rounds - 1
            even, *next_field = call(
                functools.partial(even_body, step, pairs),
                [field_shape] + [current_shape] * more,
                received + ([field_in] + past) * more,
            )
            (odd_early,) = call(odd_early_body, [field_shape], [own, current])
            for which, block in enumerate((first, second)):
                (odd_early,) = call(
                    functools.partial(odd_body, which), [field_shape], [far, block, odd_early]
                )
            mine, send = call(
                functools.partial(share_body, step, steps),
                [field_shape, current_shape],
                [even, odd_early] + [field_in] * (step >= steps),
            )
            (result,) = call(
                functools.partial(finish_body, step, steps),
                [field_shape],
                [mine, swapped(send)] + [result] * (step >= steps),
                after=collected,
            )
            field = next_field[0] if more else None
            current, going = current_in, field
    return (out, result[None])


def solution(mesh):
    placed = (
        P("delay", "surface", None, None, None),
        P("delay", "surface", None),
        P("surface", None, None),
        P(None, "surface", None),
        P("delay", "surface", None),
    )
    return jax.shard_map(
        per_device,
        mesh=mesh,
        in_specs=placed,
        out_specs=(P(None, "surface", None), P("delay", "surface", None)),
        check_vma=False,
    )
```

```python
import functools

import jax
import jax.numpy as jnp
from jax import lax
from jax.experimental import pallas as pl
from jax.experimental.pallas import tpu as pltpu
from jax.sharding import PartitionSpec as P

F32 = jnp.float32
BF16 = jnp.bfloat16
AXES = ("delay", "surface")
VMEM = pl.BlockSpec(memory_space=pltpu.VMEM)
MIB = 1024 * 1024
TOKEN = jax.ShapeDtypeStruct((8, 128), F32)


def dot(a, b):
    return jnp.dot(a, b, preferred_element_type=F32)


def place():
    lag = lax.axis_index("delay")
    return lax.rem(lag, 2), lax.div(lag, 2)


COST = pl.CostEstimate(flops=0, bytes_accessed=1 << 20, transcendentals=0)


def call(body, outs, args, after=None, in_front=None):
    specs = [VMEM] * len(args)
    if in_front is not None:
        args = args[in_front : in_front + 1] + args[:in_front] + args[in_front + 1 :]
        body = functools.partial(put_back, body, in_front)
    if after is not None:
        body = functools.partial(skip, body, len(args))
        args, specs = args + [after], specs + [pl.BlockSpec(memory_space=pl.ANY)]
    return pl.pallas_call(
        body,
        out_shape=tuple(outs),
        in_specs=specs,
        out_specs=tuple(VMEM for _ in outs),
        cost_estimate=COST,
        compiler_params=pltpu.CompilerParams(vmem_limit_bytes=8 * MIB),
    )(*args)


def only(lowest, highest, outs, body, *refs):
    _, pair = place()
    wanted = jnp.logical_and(pair >= lowest, pair <= highest)

    @pl.when(wanted)
    def _():
        body(*refs)

    @pl.when(jnp.logical_not(wanted))
    def _():
        for ref in refs[len(refs) - outs :]:
            ref[...] = jnp.zeros_like(ref)


def put_back(body, in_front, moved, *refs):
    body(*refs[:in_front], moved, *refs[in_front:])


def skip(body, number, *refs):
    body(*refs[:number], *refs[number + 1 :])


def spread_body(groups, pattern_ref, entries_ref, keep_ref, own_ref, *rest):
    *send_refs, here_ref, all_ref, slots_ref, sems, slots_sem = rest
    core, _ = place()
    blocks, slots, size, _ = entries_ref.shape
    slots_copy = pltpu.make_async_copy(pattern_ref, slots_ref, slots_sem)
    slots_copy.start()
    copies = [
        pltpu.make_async_copy(entries_ref.at[row], here_ref.at[row], sems.at[row])
        for row in range(blocks)
    ]
    for copy in copies:
        copy.start()
    base = (lax.axis_index("surface") - 2) * blocks
    total = groups * blocks
    all_ref[...] = jnp.zeros_like(all_ref)
    slots_copy.wait()
    width = 2 * blocks * size
    mine = pl.ds(pl.multiple_of(core * width, width), width)
    other = pl.ds(pl.multiple_of((1 - core) * width, width), width)
    for row in range(blocks):
        copies[row].wait()
        rows = slice(row * size, (row + 1) * size)
        for slot in range(slots):
            j = lax.rem(slots_ref[row, slot] - base + total, total)
            column = jnp.where(
                j < 2 * blocks,
                jnp.where(j < blocks, j + blocks, j - blocks),
                jnp.where(j < 3 * blocks, j + 2 * blocks, j - blocks),
            )
            columns = pl.ds(pl.multiple_of(column * size, size), size)
            all_ref[rows, columns] = here_ref[row, slot]
        keep_ref[rows, :] = all_ref[rows, mine]
        own_ref[rows, :] = all_ref[rows, 2 * width :]
        send_refs[row][...] = all_ref[rows, other]


def spread(entries, pattern, groups):
    blocks, slots, size, _ = entries.shape
    side = blocks * size

    def matrix(rows, columns):
        return jax.ShapeDtypeStruct((rows, columns), entries.dtype)

    return pl.pallas_call(
        functools.partial(spread_body, groups),
        out_shape=(matrix(side, 2 * side), matrix(side, side), *[matrix(size, 2 * side)] * blocks),
        in_specs=[pl.BlockSpec(memory_space=pl.ANY)] * 2,
        out_specs=(VMEM,) * (blocks + 2),
        scratch_shapes=[
            pltpu.VMEM(entries.shape, entries.dtype),
            pltpu.VMEM((side, 5 * side), entries.dtype),
            pltpu.SMEM(pattern.shape, pattern.dtype),
            pltpu.SemaphoreType.DMA((blocks,)),
            pltpu.SemaphoreType.DMA,
        ],
        cost_estimate=COST,
        compiler_params=pltpu.CompilerParams(vmem_limit_bytes=51 * MIB),
    )(pattern, entries)


def arrange_body(kept_ref, *rest):
    *got_refs, near_ref, far_ref = rest
    core, _ = place()

    def put(got_to_ref, kept_to_ref):
        kept_to_ref[...] = kept_ref[...]
        for i, got_ref in enumerate(got_refs):
            size = got_ref.shape[0]
            got_to_ref[i * size : (i + 1) * size, :] = got_ref[...]

    @pl.when(core == 0)
    def _():
        put(far_ref, near_ref)

    @pl.when(core == 1)
    def _():
        put(near_ref, far_ref)


def half(matrix_ref, block_ref, which):
    rows = block_ref.shape[0]
    return dot(matrix_ref[:, which * rows : (which + 1) * rows], block_ref[...])


def window(matrix_ref, first_ref, second_ref):
    return half(matrix_ref, first_ref, 0) + half(matrix_ref, second_ref, 1)


def early_body(own_ref, now_ref, *rest):
    *last, out_ref = rest
    core, _ = place()
    if last:
        far_ref, first_ref, second_ref, before_ref = last
        local = jnp.where(core == 0, now_ref[...], before_ref[...])
        out_ref[...] = dot(own_ref[...], local) + window(far_ref, first_ref, second_ref)
    else:
        local = jnp.where(core == 0, now_ref[...], jnp.zeros_like(now_ref))
        out_ref[...] = dot(own_ref[...], local)


def came(step, pairs, field_ref, history):
    core, pair = place()
    value = jnp.where(pair == pairs - 1, 0.0, field_ref[...].astype(F32))
    if history:
        mine_ref, other_ref = history
        past = jnp.where(pair == step, other_ref[...], mine_ref[...])
        special = jnp.logical_or(pair == step, pair == step + 1)
        value = jnp.where(special, jnp.where(core == 0, past, 0.0), value)
    return value


def first_body(near_ref, first_ref, early_ref, out_ref):
    out_ref[...] = early_ref[...] + half(near_ref, first_ref, 0)


def late_body(step, pairs, near_ref, second_ref, early_ref, field_ref, *rest):
    *history, out_ref = rest
    total = early_ref[...] + half(near_ref, second_ref, 1)
    out_ref[...] = (total + came(step, pairs, field_ref, history)).astype(BF16)


def even_body(step, pairs, near_ref, second_ref, early_ref, *rest):
    total = early_ref[...] + half(near_ref, second_ref, 1)
    if len(rest) == 1:
        rest[0][...] = total
        return
    field_ref, *history, even_ref, out_ref = rest
    total += came(step, pairs, field_ref, history)
    even_ref[...] = total
    out_ref[...] = total.astype(BF16)


def odd_early_body(own_ref, now_ref, out_ref):
    core, _ = place()
    out_ref[...] = dot(own_ref[...], jnp.where(core == 1, now_ref[...], jnp.zeros_like(now_ref)))


def odd_body(which, far_ref, block_ref, early_ref, out_ref):
    out_ref[...] = early_ref[...] + half(far_ref, block_ref, which)


def share_body(step, steps, even_ref, odd_ref, *rest):
    *field, keep_ref, send_ref = rest
    core, pair = place()
    even, odd = even_ref[...], odd_ref[...]
    if field:
        ended = pair == step - steps
        came_late = field[0][...].astype(F32)
        even, odd = jnp.where(ended, came_late, even), jnp.where(ended, came_late, odd)
    keep_ref[...] = jnp.where(core == 1, odd, even)
    send_ref[...] = jnp.where(core == 0, odd, even).astype(BF16)


def finish_body(step, steps, mine_ref, other_ref, *rest):
    *earlier, result_ref = rest
    core, pair = place()
    field = mine_ref[...] + other_ref[...].astype(F32)
    if earlier:
        before = earlier[0][...]
        adds = jnp.logical_and(core == 1, pair == step - steps)
        field = jnp.where(
            adds, before + field, jnp.where(pair == step - (steps - 1), field, before)
        )
    result_ref[...] = field


def collect_body(pairs, *refs):
    *seen, out_ref, token_ref = refs
    token_ref[...] = jnp.zeros_like(token_ref)
    _, pair = place()
    for step in range(out_ref.shape[0]):
        value = seen[step][...]
        for later in range(1, pairs):
            value = jnp.where(pair == later, seen[step + later][...], value)
        out_ref[step] = value


def solve(inverse_ref, rhs, out_ref, keep, other):
    size = inverse_ref.shape[1]
    fresh = []
    for i in range(inverse_ref.shape[0]):
        rows = slice(i * size, (i + 1) * size)
        block = dot(inverse_ref[i], rhs[rows]).astype(BF16)
        fresh.append(jnp.where(keep, block, other[rows]))
        out_ref[rows, :] = fresh[-1]
    return fresh


def first_history_body(history_ref, other_history_ref, out_ref):
    core, _ = place()
    out_ref[...] = jnp.where(core == 0, history_ref[...], other_history_ref[...])


def start_body(inverse_ref, excitation_ref, history_ref, out_ref):
    _, pair = place()
    rhs = (excitation_ref[0].astype(F32) - history_ref[...]).astype(BF16)
    solve(inverse_ref, rhs, out_ref, pair == 0, jnp.zeros_like(rhs))


def next_body(step, inverse_ref, excitation_ref, mine_ref, other_ref, came_ref, out_ref, going_ref):
    _, pair = place()
    field = mine_ref[...].astype(F32) + other_ref[...].astype(F32)
    rhs = (excitation_ref[step + 1].astype(F32) - field).astype(BF16)
    first_pair = pair == 0
    size = inverse_ref.shape[1]
    for i, block in enumerate(solve(inverse_ref, rhs, out_ref, first_pair, came_ref)):
        rows = slice(i * size, (i + 1) * size)
        going_ref[rows, :] = jnp.where(first_pair, block, mine_ref[rows, :])


def per_device(lagged_block_entries, pattern, diagonal_block_inverses, excitation, history):
    lags, groups = lax.axis_size("delay"), lax.axis_size("surface")
    pairs = lags // 2
    entries = lagged_block_entries[0]
    blocks, slots, size, _ = entries.shape
    steps, rows, columns = excitation.shape

    def device(d, s):
        return d * groups + s

    def everyone(move):
        return [
            (device(d, s), device(*move(d, s))) for d in range(lags) for s in range(groups)
        ]

    def swapped(value):
        return lax.ppermute(value, AXES, everyone(lambda d, s: (d ^ 1, s)))

    def pair_moved(value, hop):
        return lax.ppermute(value, AXES, everyone(lambda d, s: ((d + 2 * hop) % lags, s)))

    def halo(value, hop, since=0, until=pairs):
        def move(d, s):
            if not since <= d // 2 <= until:
                return d ^ 1, s
            return d, (s + (hop if d % 2 == 0 else -hop)) % groups

        return lax.ppermute(value, AXES, everyone(move))

    other_history = swapped(history[0])
    field_shape = jax.ShapeDtypeStruct((rows, columns), F32)
    current_shape = jax.ShapeDtypeStruct((rows, columns), BF16)
    kept, own, *sent = spread(entries, pattern[0], groups)
    (first_history,) = call(first_history_body, [field_shape], [history[0], other_history])
    (current,) = call(
        start_body,
        [current_shape],
        [diagonal_block_inverses, excitation, first_history],
    )
    matrix_shape = jax.ShapeDtypeStruct((rows, 2 * rows), kept.dtype)
    near, far = call(arrange_body, [matrix_shape, matrix_shape], [kept] + [swapped(part) for part in sent])

    going = field = current
    seen = []
    previous = []
    result = None
    out = collected = None
    rounds = steps + pairs - 1
    windows = None
    for step in range(rounds):
        seen.append(current)
        if step == rounds - 1:
            out, collected = call(
                functools.partial(collect_body, pairs),
                [jax.ShapeDtypeStruct(excitation.shape, BF16), TOKEN],
                seen,
            )
        first, second = windows or (halo(current, 1, 0, step), halo(current, 2, 0, step))
        if pairs == 2:
            current_in = field_in = pair_moved(going, 1)
        else:
            current_in, field_in = pair_moved(current, 1), pair_moved(field, -1)
        last = [far, *previous] if previous else []
        ending = max(step - (steps - 1), 0)
        going_on = functools.partial(only, ending, pairs)
        (early,) = call(
            functools.partial(going_on, 1, early_body), [field_shape], [own, current] + last
        )
        (partly,) = call(
            functools.partial(going_on, 1, first_body), [field_shape], [near, first, early]
        )
        received = [near, second, partly]
        past = [history[0], other_history] if step < pairs else []
        previous = [first, second, current]
        if step < steps - 1:
            (field,) = call(
                functools.partial(late_body, step, pairs),
                [current_shape],
                received + [field_in] + past,
                in_front=len(received) if step == 1 else None,
            )
            current, going = call(
                functools.partial(next_body, step),
                [current_shape, current_shape],
                [diagonal_block_inverses, excitation, field, swapped(field), current_in],
            )
        else:
            if step < rounds - 1:
                done = step + 2 - steps
                windows = halo(current_in, 1, done), halo(current_in, 2, done)
            more = step < rounds - 1
            even, *next_field = call(
                functools.partial(going_on, 1 + more, functools.partial(even_body, step, pairs)),
                [field_shape] + [current_shape] * more,
                received + ([field_in] + past) * more,
            )
            alone = functools.partial(only, ending, ending, 1)
            (odd_early,) = call(
                functools.partial(alone, odd_early_body), [field_shape], [own, current]
            )
            for which, block in enumerate((first, second)):
                (odd_early,) = call(
                    functools.partial(alone, functools.partial(odd_body, which)),
                    [field_shape],
                    [far, block, odd_early],
                )
            mine, send = call(
                functools.partial(share_body, step, steps),
                [field_shape, current_shape],
                [even, odd_early] + [field_in] * (step >= steps),
            )
            (result,) = call(
                functools.partial(finish_body, step, steps),
                [field_shape],
                [mine, swapped(send)] + [result] * (step >= steps),
                after=collected,
            )
            field = next_field[0] if more else None
            current, going = current_in, field
    return (out, result[None])


def solution(mesh):
    placed = (
        P("delay", "surface", None, None, None),
        P("delay", "surface", None),
        P("surface", None, None),
        P(None, "surface", None),
        P("delay", "surface", None),
    )
    return jax.shard_map(
        per_device,
        mesh=mesh,
        in_specs=placed,
        out_specs=(P(None, "surface", None), P("delay", "surface", None)),
        check_vma=False,
    )
```

```python
import functools

import jax
import jax.numpy as jnp
from jax import lax
from jax.experimental import pallas as pl
from jax.experimental.pallas import tpu as pltpu
from jax.sharding import PartitionSpec as P

F32 = jnp.float32
BF16 = jnp.bfloat16
AXES = ("delay", "surface")
VMEM = pl.BlockSpec(memory_space=pltpu.VMEM)
MIB = 1024 * 1024
TOKEN = jax.ShapeDtypeStruct((8, 128), F32)


def dot(a, b):
    return jnp.dot(a, b, preferred_element_type=F32)


def place():
    lag = lax.axis_index("delay")
    return lax.rem(lag, 2), lax.div(lag, 2)


COST = pl.CostEstimate(flops=0, bytes_accessed=1 << 20, transcendentals=0)


def call(body, outs, args, after=None, in_front=None):
    specs = [VMEM] * len(args)
    if in_front is not None:
        args = args[in_front : in_front + 1] + args[:in_front] + args[in_front + 1 :]
        body = functools.partial(put_back, body, in_front)
    if after is not None:
        body = functools.partial(skip, body, len(args))
        args, specs = args + [after], specs + [pl.BlockSpec(memory_space=pl.ANY)]
    return pl.pallas_call(
        body,
        out_shape=tuple(outs),
        in_specs=specs,
        out_specs=tuple(VMEM for _ in outs),
        cost_estimate=COST,
        compiler_params=pltpu.CompilerParams(vmem_limit_bytes=8 * MIB),
    )(*args)


def only(lowest, highest, outs, body, *refs):
    _, pair = place()
    wanted = jnp.logical_and(pair >= lowest, pair <= highest)

    @pl.when(wanted)
    def _():
        body(*refs)

    @pl.when(jnp.logical_not(wanted))
    def _():
        for ref in refs[len(refs) - outs :]:
            ref[...] = jnp.zeros_like(ref)


def put_back(body, in_front, moved, *refs):
    body(*refs[:in_front], moved, *refs[in_front:])


def skip(body, number, *refs):
    body(*refs[:number], *refs[number + 1 :])


def spread_body(groups, pattern_ref, entries_ref, keep_ref, own_ref, *rest):
    *send_refs, here_ref, all_ref, slots_ref, sems, slots_sem = rest
    core, _ = place()
    blocks, slots, size, _ = entries_ref.shape
    slots_copy = pltpu.make_async_copy(pattern_ref, slots_ref, slots_sem)
    slots_copy.start()
    copies = [
        pltpu.make_async_copy(entries_ref.at[row], here_ref.at[row], sems.at[row])
        for row in range(blocks)
    ]
    for copy in copies:
        copy.start()
    base = (lax.axis_index("surface") - 2) * blocks
    total = groups * blocks
    all_ref[...] = jnp.zeros_like(all_ref)
    slots_copy.wait()
    width = 2 * blocks * size
    mine = pl.ds(pl.multiple_of(core * width, width), width)
    other = pl.ds(pl.multiple_of((1 - core) * width, width), width)
    for row in range(blocks):
        copies[row].wait()
        rows = slice(row * size, (row + 1) * size)
        for slot in range(slots):
            j = lax.rem(slots_ref[row, slot] - base + total, total)
            column = jnp.where(
                j < 2 * blocks,
                jnp.where(j < blocks, j + blocks, j - blocks),
                jnp.where(j < 3 * blocks, j + 2 * blocks, j - blocks),
            )
            columns = pl.ds(pl.multiple_of(column * size, size), size)
            all_ref[rows, columns] = here_ref[row, slot]
        keep_ref[rows, :] = all_ref[rows, mine]
        own_ref[rows, :] = all_ref[rows, 2 * width :]
        send_refs[row][...] = all_ref[rows, other]


def spread(entries, pattern, groups):
    blocks, slots, size, _ = entries.shape
    side = blocks * size

    def matrix(rows, columns):
        return jax.ShapeDtypeStruct((rows, columns), entries.dtype)

    return pl.pallas_call(
        functools.partial(spread_body, groups),
        out_shape=(matrix(side, 2 * side), matrix(side, side), *[matrix(size, 2 * side)] * blocks),
        in_specs=[pl.BlockSpec(memory_space=pl.ANY)] * 2,
        out_specs=(VMEM,) * (blocks + 2),
        scratch_shapes=[
            pltpu.VMEM(entries.shape, entries.dtype),
            pltpu.VMEM((side, 5 * side), entries.dtype),
            pltpu.SMEM(pattern.shape, pattern.dtype),
            pltpu.SemaphoreType.DMA((blocks,)),
            pltpu.SemaphoreType.DMA,
        ],
        cost_estimate=COST,
        compiler_params=pltpu.CompilerParams(vmem_limit_bytes=51 * MIB),
    )(pattern, entries)


def arrange_body(kept_ref, *rest):
    *got_refs, near_ref, far_ref = rest
    core, _ = place()

    def put(got_to_ref, kept_to_ref):
        kept_to_ref[...] = kept_ref[...]
        for i, got_ref in enumerate(got_refs):
            size = got_ref.shape[0]
            got_to_ref[i * size : (i + 1) * size, :] = got_ref[...]

    @pl.when(core == 0)
    def _():
        put(far_ref, near_ref)

    @pl.when(core == 1)
    def _():
        put(near_ref, far_ref)


def half(matrix_ref, block_ref, which):
    rows = block_ref.shape[0]
    return dot(matrix_ref[:, which * rows : (which + 1) * rows], block_ref[...])


def window(matrix_ref, first_ref, second_ref):
    return half(matrix_ref, first_ref, 0) + half(matrix_ref, second_ref, 1)


def early_body(own_ref, now_ref, *rest):
    *last, out_ref = rest
    core, _ = place()
    if last:
        far_ref, first_ref, second_ref, before_ref = last
        local = jnp.where(core == 0, now_ref[...], before_ref[...])
        out_ref[...] = dot(own_ref[...], local) + window(far_ref, first_ref, second_ref)
    else:
        local = jnp.where(core == 0, now_ref[...], jnp.zeros_like(now_ref))
        out_ref[...] = dot(own_ref[...], local)


def came(step, pairs, field_ref, history):
    core, pair = place()
    value = jnp.where(pair == pairs - 1, 0.0, field_ref[...].astype(F32))
    if history:
        mine_ref, other_ref = history
        past = jnp.where(pair == step, other_ref[...], mine_ref[...])
        special = jnp.logical_or(pair == step, pair == step + 1)
        value = jnp.where(special, jnp.where(core == 0, past, 0.0), value)
    return value


def first_body(near_ref, first_ref, early_ref, out_ref):
    out_ref[...] = early_ref[...] + half(near_ref, first_ref, 0)


def late_body(step, pairs, near_ref, second_ref, early_ref, field_ref, *rest):
    *history, out_ref = rest
    total = early_ref[...] + half(near_ref, second_ref, 1)
    out_ref[...] = total + came(step, pairs, field_ref, history)


def even_body(step, pairs, near_ref, second_ref, early_ref, *rest):
    total = early_ref[...] + half(near_ref, second_ref, 1)
    if len(rest) == 1:
        rest[0][...] = total
        return
    field_ref, *history, even_ref, out_ref = rest
    total += came(step, pairs, field_ref, history)
    even_ref[...] = total
    out_ref[...] = total.astype(BF16)


def odd_early_body(own_ref, now_ref, out_ref):
    core, _ = place()
    out_ref[...] = dot(own_ref[...], jnp.where(core == 1, now_ref[...], jnp.zeros_like(now_ref)))


def odd_body(which, far_ref, block_ref, early_ref, out_ref):
    out_ref[...] = early_ref[...] + half(far_ref, block_ref, which)


def share_body(step, steps, even_ref, odd_ref, *rest):
    *field, keep_ref, send_ref = rest
    core, pair = place()
    even, odd = even_ref[...], odd_ref[...]
    if field:
        ended = pair == step - steps
        came_late = field[0][...].astype(F32)
        even, odd = jnp.where(ended, came_late, even), jnp.where(ended, came_late, odd)
    keep_ref[...] = jnp.where(core == 1, odd, even)
    send_ref[...] = jnp.where(core == 0, odd, even).astype(BF16)


def finish_body(step, steps, mine_ref, other_ref, *rest):
    *earlier, result_ref = rest
    core, pair = place()
    field = mine_ref[...] + other_ref[...].astype(F32)
    if earlier:
        before = earlier[0][...]
        adds = jnp.logical_and(core == 1, pair == step - steps)
        field = jnp.where(
            adds, before + field, jnp.where(pair == step - (steps - 1), field, before)
        )
    result_ref[...] = field


def collect_body(pairs, *refs):
    *seen, out_ref, token_ref = refs
    token_ref[...] = jnp.zeros_like(token_ref)
    _, pair = place()
    for step in range(out_ref.shape[0]):
        value = seen[step][...]
        for later in range(1, pairs):
            value = jnp.where(pair == later, seen[step + later][...], value)
        out_ref[step] = value


def solve(inverse_ref, rhs, out_ref, keep, other):
    size = inverse_ref.shape[1]
    fresh = []
    for i in range(inverse_ref.shape[0]):
        rows = slice(i * size, (i + 1) * size)
        block = dot(inverse_ref[i], rhs[rows]).astype(BF16)
        fresh.append(jnp.where(keep, block, other[rows]))
        out_ref[rows, :] = fresh[-1]
    return fresh


def first_history_body(history_ref, other_history_ref, out_ref):
    core, _ = place()
    out_ref[...] = jnp.where(core == 0, history_ref[...], other_history_ref[...])


def start_body(inverse_ref, excitation_ref, history_ref, out_ref):
    _, pair = place()
    rhs = (excitation_ref[0].astype(F32) - history_ref[...]).astype(BF16)
    solve(inverse_ref, rhs, out_ref, pair == 0, jnp.zeros_like(rhs))


def next_body(step, inverse_ref, excitation_ref, mine_ref, other_ref, came_ref, out_ref, going_ref):
    _, pair = place()
    field = mine_ref[...] + other_ref[...]
    rhs = (excitation_ref[step + 1].astype(F32) - field).astype(BF16)
    first_pair = pair == 0
    size = inverse_ref.shape[1]
    for i, block in enumerate(solve(inverse_ref, rhs, out_ref, first_pair, came_ref)):
        rows = slice(i * size, (i + 1) * size)
        going_ref[rows, :] = jnp.where(first_pair, block, mine_ref[rows, :].astype(BF16))


def per_device(lagged_block_entries, pattern, diagonal_block_inverses, excitation, history):
    lags, groups = lax.axis_size("delay"), lax.axis_size("surface")
    pairs = lags // 2
    entries = lagged_block_entries[0]
    blocks, slots, size, _ = entries.shape
    steps, rows, columns = excitation.shape

    def device(d, s):
        return d * groups + s

    def everyone(move):
        return [
            (device(d, s), device(*move(d, s))) for d in range(lags) for s in range(groups)
        ]

    def swapped(value):
        return lax.ppermute(value, AXES, everyone(lambda d, s: (d ^ 1, s)))

    def pair_moved(value, hop):
        return lax.ppermute(value, AXES, everyone(lambda d, s: ((d + 2 * hop) % lags, s)))

    def halo(value, hop, since=0, until=pairs):
        def move(d, s):
            if not since <= d // 2 <= until:
                return d ^ 1, s
            return d, (s + (hop if d % 2 == 0 else -hop)) % groups

        return lax.ppermute(value, AXES, everyone(move))

    other_history = swapped(history[0])
    field_shape = jax.ShapeDtypeStruct((rows, columns), F32)
    current_shape = jax.ShapeDtypeStruct((rows, columns), BF16)
    kept, own, *sent = spread(entries, pattern[0], groups)
    (first_history,) = call(first_history_body, [field_shape], [history[0], other_history])
    (current,) = call(
        start_body,
        [current_shape],
        [diagonal_block_inverses, excitation, first_history],
    )
    matrix_shape = jax.ShapeDtypeStruct((rows, 2 * rows), kept.dtype)
    near, far = call(arrange_body, [matrix_shape, matrix_shape], [kept] + [swapped(part) for part in sent])

    going = field = current
    seen = []
    previous = []
    result = None
    out = collected = None
    rounds = steps + pairs - 1
    windows = None
    for step in range(rounds):
        seen.append(current)
        if step == rounds - 1:
            out, collected = call(
                functools.partial(collect_body, pairs),
                [jax.ShapeDtypeStruct(excitation.shape, BF16), TOKEN],
                seen,
            )
        first, second = windows or (halo(current, 1, 0, step), halo(current, 2, 0, step))
        if pairs == 2:
            current_in = field_in = pair_moved(going, 1)
        else:
            current_in, field_in = pair_moved(current, 1), pair_moved(field.astype(BF16), -1)
        last = [far, *previous] if previous else []
        ending = max(step - (steps - 1), 0)
        going_on = functools.partial(only, ending, pairs)
        (early,) = call(
            functools.partial(going_on, 1, early_body), [field_shape], [own, current] + last
        )
        (partly,) = call(
            functools.partial(going_on, 1, first_body), [field_shape], [near, first, early]
        )
        received = [near, second, partly]
        past = [history[0], other_history] if step < pairs else []
        previous = [first, second, current]
        if step < steps - 1:
            (field,) = call(
                functools.partial(late_body, step, pairs),
                [field_shape],
                received + [field_in] + past,
                in_front=len(received) if step == 1 else None,
            )
            current, going = call(
                functools.partial(next_body, step),
                [current_shape, current_shape],
                [diagonal_block_inverses, excitation, field, swapped(field), current_in],
            )
        else:
            if step < rounds - 1:
                done = step + 2 - steps
                windows = halo(current_in, 1, done), halo(current_in, 2, done)
            more = step < rounds - 1
            even, *next_field = call(
                functools.partial(going_on, 1 + more, functools.partial(even_body, step, pairs)),
                [field_shape] + [current_shape] * more,
                received + ([field_in] + past) * more,
            )
            alone = functools.partial(only, ending, ending, 1)
            (odd_early,) = call(
                functools.partial(alone, odd_early_body), [field_shape], [own, current]
            )
            for which, block in enumerate((first, second)):
                (odd_early,) = call(
                    functools.partial(alone, functools.partial(odd_body, which)),
                    [field_shape],
                    [far, block, odd_early],
                )
            mine, send = call(
                functools.partial(share_body, step, steps),
                [field_shape, current_shape],
                [even, odd_early] + [field_in] * (step >= steps),
            )
            (result,) = call(
                functools.partial(finish_body, step, steps),
                [field_shape],
                [mine, swapped(send)] + [result] * (step >= steps),
                after=collected,
            )
            field = next_field[0] if more else None
            current, going = current_in, field
    return (out, result[None])


def solution(mesh):
    placed = (
        P("delay", "surface", None, None, None),
        P("delay", "surface", None),
        P("surface", None, None),
        P(None, "surface", None),
        P("delay", "surface", None),
    )
    return jax.shard_map(
        per_device,
        mesh=mesh,
        in_specs=placed,
        out_specs=(P(None, "surface", None), P("delay", "surface", None)),
        check_vma=False,
    )
```

```python
import functools

import jax
import jax.numpy as jnp
from jax import lax
from jax.experimental import pallas as pl
from jax.experimental.pallas import tpu as pltpu
from jax.sharding import PartitionSpec as P

F32 = jnp.float32
BF16 = jnp.bfloat16
AXES = ("delay", "surface")
VMEM = pl.BlockSpec(memory_space=pltpu.VMEM)
MIB = 1024 * 1024
CHUNKS = 2
TOKEN = jax.ShapeDtypeStruct((8, 128), F32)


def dot(a, b):
    return jnp.dot(a, b, preferred_element_type=F32)


def place():
    lag = lax.axis_index("delay")
    return lax.rem(lag, 2), lax.div(lag, 2)


COST = pl.CostEstimate(flops=0, bytes_accessed=1 << 20, transcendentals=0)


def call(body, outs, args, after=None, in_front=None):
    specs = [VMEM] * len(args)
    if in_front is not None:
        args = args[in_front : in_front + 1] + args[:in_front] + args[in_front + 1 :]
        body = functools.partial(put_back, body, in_front)
    if after is not None:
        body = functools.partial(skip, body, len(args))
        args, specs = args + [after], specs + [pl.BlockSpec(memory_space=pl.ANY)]
    return pl.pallas_call(
        body,
        out_shape=tuple(outs),
        in_specs=specs,
        out_specs=tuple(VMEM for _ in outs),
        cost_estimate=COST,
        compiler_params=pltpu.CompilerParams(vmem_limit_bytes=8 * MIB),
    )(*args)


def only(lowest, highest, outs, body, *refs):
    _, pair = place()
    wanted = jnp.logical_and(pair >= lowest, pair <= highest)

    @pl.when(wanted)
    def _():
        body(*refs)

    @pl.when(jnp.logical_not(wanted))
    def _():
        for ref in refs[len(refs) - outs :]:
            ref[...] = jnp.zeros_like(ref)


def put_back(body, in_front, moved, *refs):
    body(*refs[:in_front], moved, *refs[in_front:])


def skip(body, number, *refs):
    body(*refs[:number], *refs[number + 1 :])


def spread_body(groups, pattern_ref, entries_ref, keep_ref, own_ref, *rest):
    *send_refs, here_ref, all_ref, slots_ref, sems, slots_sem = rest
    core, _ = place()
    blocks, slots, size, _ = entries_ref.shape
    slots_copy = pltpu.make_async_copy(pattern_ref, slots_ref, slots_sem)
    slots_copy.start()
    copies = [
        pltpu.make_async_copy(entries_ref.at[row], here_ref.at[row], sems.at[row])
        for row in range(blocks)
    ]
    for copy in copies:
        copy.start()
    base = (lax.axis_index("surface") - 2) * blocks
    total = groups * blocks
    all_ref[...] = jnp.zeros_like(all_ref)
    slots_copy.wait()
    width = 2 * blocks * size
    mine = pl.ds(pl.multiple_of(core * width, width), width)
    other = pl.ds(pl.multiple_of((1 - core) * width, width), width)
    for row in range(blocks):
        copies[row].wait()
        rows = slice(row * size, (row + 1) * size)
        for slot in range(slots):
            j = lax.rem(slots_ref[row, slot] - base + total, total)
            column = jnp.where(
                j < 2 * blocks,
                jnp.where(j < blocks, j + blocks, j - blocks),
                jnp.where(j < 3 * blocks, j + 2 * blocks, j - blocks),
            )
            columns = pl.ds(pl.multiple_of(column * size, size), size)
            all_ref[rows, columns] = here_ref[row, slot]
        keep_ref[rows, :] = all_ref[rows, mine]
        own_ref[rows, :] = all_ref[rows, 2 * width :]
        send_refs[row][...] = all_ref[rows, other]


def spread(entries, pattern, groups):
    blocks, slots, size, _ = entries.shape
    side = blocks * size

    def matrix(rows, columns):
        return jax.ShapeDtypeStruct((rows, columns), entries.dtype)

    return pl.pallas_call(
        functools.partial(spread_body, groups),
        out_shape=(matrix(side, 2 * side), matrix(side, side), *[matrix(size, 2 * side)] * blocks),
        in_specs=[pl.BlockSpec(memory_space=pl.ANY)] * 2,
        out_specs=(VMEM,) * (blocks + 2),
        scratch_shapes=[
            pltpu.VMEM(entries.shape, entries.dtype),
            pltpu.VMEM((side, 5 * side), entries.dtype),
            pltpu.SMEM(pattern.shape, pattern.dtype),
            pltpu.SemaphoreType.DMA((blocks,)),
            pltpu.SemaphoreType.DMA,
        ],
        cost_estimate=COST,
        compiler_params=pltpu.CompilerParams(vmem_limit_bytes=51 * MIB),
    )(pattern, entries)


def arrange_body(kept_ref, *rest):
    *got_refs, near_ref, far_ref = rest
    core, _ = place()

    def put(got_to_ref, kept_to_ref):
        kept_to_ref[...] = kept_ref[...]
        for i, got_ref in enumerate(got_refs):
            size = got_ref.shape[0]
            got_to_ref[i * size : (i + 1) * size, :] = got_ref[...]

    @pl.when(core == 0)
    def _():
        put(far_ref, near_ref)

    @pl.when(core == 1)
    def _():
        put(near_ref, far_ref)


def half(matrix_ref, block_ref, which):
    rows = block_ref.shape[0]
    return dot(matrix_ref[:, which * rows : (which + 1) * rows], block_ref[...])


def window(matrix_ref, first_ref, second_ref):
    return half(matrix_ref, first_ref, 0) + half(matrix_ref, second_ref, 1)


def early_body(own_ref, now_ref, *rest):
    *last, out_ref = rest
    core, _ = place()
    if last:
        far_ref, first_ref, second_ref, before_ref = last
        local = jnp.where(core == 0, now_ref[...], before_ref[...])
        out_ref[...] = dot(own_ref[...], local) + window(far_ref, first_ref, second_ref)
    else:
        local = jnp.where(core == 0, now_ref[...], jnp.zeros_like(now_ref))
        out_ref[...] = dot(own_ref[...], local)


def came(step, pairs, field_ref, history):
    core, pair = place()
    value = jnp.where(pair == pairs - 1, 0.0, field_ref[...].astype(F32))
    if history:
        mine_ref, other_ref = history
        past = jnp.where(pair == step, other_ref[...], mine_ref[...])
        special = jnp.logical_or(pair == step, pair == step + 1)
        value = jnp.where(special, jnp.where(core == 0, past, 0.0), value)
    return value


def add_half(matrix_ref, block_ref, which, early_ref, put):
    rows = block_ref.shape[0]
    size = rows // CHUNKS
    block = block_ref[...]
    columns = slice(which * rows, (which + 1) * rows)
    for i in range(CHUNKS):
        part = slice(i * size, (i + 1) * size)
        put(part, early_ref[part, :] + dot(matrix_ref[part, columns], block))


def first_body(near_ref, first_ref, early_ref, out_ref):
    def put(part, total):
        out_ref[part, :] = total

    add_half(near_ref, first_ref, 0, early_ref, put)


def late_body(step, pairs, near_ref, second_ref, early_ref, field_ref, *rest):
    *history, out_ref = rest
    value = came(step, pairs, field_ref, history)

    def put(part, total):
        out_ref[part, :] = (total + value[part]).astype(BF16)

    add_half(near_ref, second_ref, 1, early_ref, put)


def even_body(step, pairs, near_ref, second_ref, early_ref, *rest):
    total = early_ref[...] + half(near_ref, second_ref, 1)
    if len(rest) == 1:
        rest[0][...] = total
        return
    field_ref, *history, even_ref, out_ref = rest
    total += came(step, pairs, field_ref, history)
    even_ref[...] = total
    out_ref[...] = total.astype(BF16)


def odd_early_body(own_ref, now_ref, out_ref):
    core, _ = place()
    out_ref[...] = dot(own_ref[...], jnp.where(core == 1, now_ref[...], jnp.zeros_like(now_ref)))


def odd_body(which, far_ref, block_ref, early_ref, out_ref):
    out_ref[...] = early_ref[...] + half(far_ref, block_ref, which)


def share_body(step, steps, even_ref, odd_ref, *rest):
    *field, keep_ref, send_ref = rest
    core, pair = place()
    even, odd = even_ref[...], odd_ref[...]
    if field:
        ended = pair == step - steps
        came_late = field[0][...].astype(F32)
        even, odd = jnp.where(ended, came_late, even), jnp.where(ended, came_late, odd)
    keep_ref[...] = jnp.where(core == 1, odd, even)
    send_ref[...] = jnp.where(core == 0, odd, even).astype(BF16)


def finish_body(step, steps, mine_ref, other_ref, *rest):
    *earlier, result_ref = rest
    core, pair = place()
    field = mine_ref[...] + other_ref[...].astype(F32)
    if earlier:
        before = earlier[0][...]
        adds = jnp.logical_and(core == 1, pair == step - steps)
        field = jnp.where(
            adds, before + field, jnp.where(pair == step - (steps - 1), field, before)
        )
    result_ref[...] = field


def collect_body(pairs, *refs):
    *seen, out_ref, token_ref = refs
    token_ref[...] = jnp.zeros_like(token_ref)
    _, pair = place()
    for step in range(out_ref.shape[0]):
        value = seen[step][...]
        for later in range(1, pairs):
            value = jnp.where(pair == later, seen[step + later][...], value)
        out_ref[step] = value


def solve(inverse_ref, rhs, out_ref, keep, other):
    size = inverse_ref.shape[1]
    fresh = []
    for i in range(inverse_ref.shape[0]):
        rows = slice(i * size, (i + 1) * size)
        block = dot(inverse_ref[i], rhs[rows]).astype(BF16)
        fresh.append(jnp.where(keep, block, other[rows]))
        out_ref[rows, :] = fresh[-1]
    return fresh


def first_history_body(history_ref, other_history_ref, out_ref):
    core, _ = place()
    out_ref[...] = jnp.where(core == 0, history_ref[...], other_history_ref[...])


def start_body(inverse_ref, excitation_ref, history_ref, out_ref):
    _, pair = place()
    rhs = (excitation_ref[0].astype(F32) - history_ref[...]).astype(BF16)
    solve(inverse_ref, rhs, out_ref, pair == 0, jnp.zeros_like(rhs))


def next_body(step, inverse_ref, excitation_ref, mine_ref, other_ref, came_ref, out_ref, going_ref):
    _, pair = place()
    field = mine_ref[...].astype(F32) + other_ref[...].astype(F32)
    rhs = (excitation_ref[step + 1].astype(F32) - field).astype(BF16)
    first_pair = pair == 0
    size = inverse_ref.shape[1]
    for i, block in enumerate(solve(inverse_ref, rhs, out_ref, first_pair, came_ref)):
        rows = slice(i * size, (i + 1) * size)
        going_ref[rows, :] = jnp.where(first_pair, block, mine_ref[rows, :])


def per_device(lagged_block_entries, pattern, diagonal_block_inverses, excitation, history):
    lags, groups = lax.axis_size("delay"), lax.axis_size("surface")
    pairs = lags // 2
    entries = lagged_block_entries[0]
    blocks, slots, size, _ = entries.shape
    steps, rows, columns = excitation.shape

    def device(d, s):
        return d * groups + s

    def everyone(move):
        return [
            (device(d, s), device(*move(d, s))) for d in range(lags) for s in range(groups)
        ]

    def swapped(value):
        return lax.ppermute(value, AXES, everyone(lambda d, s: (d ^ 1, s)))

    def pair_moved(value, hop):
        return lax.ppermute(value, AXES, everyone(lambda d, s: ((d + 2 * hop) % lags, s)))

    def halo(value, hop, since=0, until=pairs):
        def move(d, s):
            if not since <= d // 2 <= until:
                return d ^ 1, s
            return d, (s + (hop if d % 2 == 0 else -hop)) % groups

        return lax.ppermute(value, AXES, everyone(move))

    other_history = swapped(history[0])
    field_shape = jax.ShapeDtypeStruct((rows, columns), F32)
    current_shape = jax.ShapeDtypeStruct((rows, columns), BF16)
    kept, own, *sent = spread(entries, pattern[0], groups)
    (first_history,) = call(first_history_body, [field_shape], [history[0], other_history])
    (current,) = call(
        start_body,
        [current_shape],
        [diagonal_block_inverses, excitation, first_history],
    )
    matrix_shape = jax.ShapeDtypeStruct((rows, 2 * rows), kept.dtype)
    near, far = call(arrange_body, [matrix_shape, matrix_shape], [kept] + [swapped(part) for part in sent])

    going = field = current
    seen = []
    previous = []
    result = None
    out = collected = None
    rounds = steps + pairs - 1
    windows = None
    for step in range(rounds):
        seen.append(current)
        if step == rounds - 1:
            out, collected = call(
                functools.partial(collect_body, pairs),
                [jax.ShapeDtypeStruct(excitation.shape, BF16), TOKEN],
                seen,
            )
        first, second = windows or (halo(current, 1, 0, step), halo(current, 2, 0, step))
        if pairs == 2:
            current_in = field_in = pair_moved(going, 1)
        else:
            current_in, field_in = pair_moved(current, 1), pair_moved(field, -1)
        last = [far, *previous] if previous else []
        ending = max(step - (steps - 1), 0)
        going_on = functools.partial(only, ending, pairs)
        (early,) = call(
            functools.partial(going_on, 1, early_body), [field_shape], [own, current] + last
        )
        (partly,) = call(
            functools.partial(going_on, 1, first_body), [field_shape], [near, first, early]
        )
        received = [near, second, partly]
        past = [history[0], other_history] if step < pairs else []
        previous = [first, second, current]
        if step < steps - 1:
            (field,) = call(
                functools.partial(late_body, step, pairs),
                [current_shape],
                received + [field_in] + past,
                in_front=len(received) if step == 1 else None,
            )
            current, going = call(
                functools.partial(next_body, step),
                [current_shape, current_shape],
                [diagonal_block_inverses, excitation, field, swapped(field), current_in],
            )
        else:
            if step < rounds - 1:
                done = step + 2 - steps
                windows = halo(current_in, 1, done), halo(current_in, 2, done)
            more = step < rounds - 1
            even, *next_field = call(
                functools.partial(going_on, 1 + more, functools.partial(even_body, step, pairs)),
                [field_shape] + [current_shape] * more,
                received + ([field_in] + past) * more,
            )
            alone = functools.partial(only, ending, ending, 1)
            (odd_early,) = call(
                functools.partial(alone, odd_early_body), [field_shape], [own, current]
            )
            for which, block in enumerate((first, second)):
                (odd_early,) = call(
                    functools.partial(alone, functools.partial(odd_body, which)),
                    [field_shape],
                    [far, block, odd_early],
                )
            mine, send = call(
                functools.partial(share_body, step, steps),
                [field_shape, current_shape],
                [even, odd_early] + [field_in] * (step >= steps),
            )
            (result,) = call(
                functools.partial(finish_body, step, steps),
                [field_shape],
                [mine, swapped(send)] + [result] * (step >= steps),
                after=collected,
            )
            field = next_field[0] if more else None
            current, going = current_in, field
    return (out, result[None])


def solution(mesh):
    placed = (
        P("delay", "surface", None, None, None),
        P("delay", "surface", None),
        P("surface", None, None),
        P(None, "surface", None),
        P("delay", "surface", None),
    )
    return jax.shard_map(
        per_device,
        mesh=mesh,
        in_specs=placed,
        out_specs=(P(None, "surface", None), P("delay", "surface", None)),
        check_vma=False,
    )
```

```python
import functools

import jax
import jax.numpy as jnp
from jax import lax
from jax.experimental import pallas as pl
from jax.experimental.pallas import tpu as pltpu
from jax.sharding import PartitionSpec as P

F32 = jnp.float32
BF16 = jnp.bfloat16
AXES = ("delay", "surface")
VMEM = pl.BlockSpec(memory_space=pltpu.VMEM)
MIB = 1024 * 1024
CHUNKS = 2
TOKEN = jax.ShapeDtypeStruct((8, 128), F32)


def dot(a, b):
    return jnp.dot(a, b, preferred_element_type=F32)


def place():
    lag = lax.axis_index("delay")
    return lax.rem(lag, 2), lax.div(lag, 2)


COST = pl.CostEstimate(flops=0, bytes_accessed=1 << 20, transcendentals=0)


def call(body, outs, args, after=None, in_front=None):
    specs = [VMEM] * len(args)
    if in_front is not None:
        args = args[in_front : in_front + 1] + args[:in_front] + args[in_front + 1 :]
        body = functools.partial(put_back, body, in_front)
    if after is not None:
        body = functools.partial(skip, body, len(args))
        args, specs = args + [after], specs + [pl.BlockSpec(memory_space=pl.ANY)]
    return pl.pallas_call(
        body,
        out_shape=tuple(outs),
        in_specs=specs,
        out_specs=tuple(VMEM for _ in outs),
        cost_estimate=COST,
        compiler_params=pltpu.CompilerParams(vmem_limit_bytes=8 * MIB),
    )(*args)


def only(lowest, highest, outs, body, *refs):
    _, pair = place()
    wanted = jnp.logical_and(pair >= lowest, pair <= highest)

    @pl.when(wanted)
    def _():
        body(*refs)

    @pl.when(jnp.logical_not(wanted))
    def _():
        for ref in refs[len(refs) - outs :]:
            ref[...] = jnp.zeros_like(ref)


def put_back(body, in_front, moved, *refs):
    body(*refs[:in_front], moved, *refs[in_front:])


def skip(body, number, *refs):
    body(*refs[:number], *refs[number + 1 :])


def spread_body(groups, pattern_ref, entries_ref, keep_ref, own_ref, *rest):
    *send_refs, here_ref, all_ref, slots_ref, sems, slots_sem = rest
    core, _ = place()
    blocks, slots, size, _ = entries_ref.shape
    slots_copy = pltpu.make_async_copy(pattern_ref, slots_ref, slots_sem)
    slots_copy.start()
    copies = [
        pltpu.make_async_copy(entries_ref.at[row], here_ref.at[row], sems.at[row])
        for row in range(blocks)
    ]
    for copy in copies:
        copy.start()
    base = (lax.axis_index("surface") - 2) * blocks
    total = groups * blocks
    all_ref[...] = jnp.zeros_like(all_ref)
    slots_copy.wait()
    width = 2 * blocks * size
    mine = pl.ds(pl.multiple_of(core * width, width), width)
    other = pl.ds(pl.multiple_of((1 - core) * width, width), width)
    for row in range(blocks):
        copies[row].wait()
        rows = slice(row * size, (row + 1) * size)
        for slot in range(slots):
            j = lax.rem(slots_ref[row, slot] - base + total, total)
            column = jnp.where(
                j < 2 * blocks,
                jnp.where(j < blocks, j + blocks, j - blocks),
                jnp.where(j < 3 * blocks, j + 2 * blocks, j - blocks),
            )
            columns = pl.ds(pl.multiple_of(column * size, size), size)
            all_ref[rows, columns] = here_ref[row, slot]
        keep_ref[rows, :] = all_ref[rows, mine]
        own_ref[rows, :] = all_ref[rows, 2 * width :]
        send_refs[row][...] = all_ref[rows, other]


def spread(entries, pattern, groups):
    blocks, slots, size, _ = entries.shape
    side = blocks * size

    def matrix(rows, columns):
        return jax.ShapeDtypeStruct((rows, columns), entries.dtype)

    return pl.pallas_call(
        functools.partial(spread_body, groups),
        out_shape=(matrix(side, 2 * side), matrix(side, side), *[matrix(size, 2 * side)] * blocks),
        in_specs=[pl.BlockSpec(memory_space=pl.ANY)] * 2,
        out_specs=(VMEM,) * (blocks + 2),
        scratch_shapes=[
            pltpu.VMEM(entries.shape, entries.dtype),
            pltpu.VMEM((side, 5 * side), entries.dtype),
            pltpu.SMEM(pattern.shape, pattern.dtype),
            pltpu.SemaphoreType.DMA((blocks,)),
            pltpu.SemaphoreType.DMA,
        ],
        cost_estimate=COST,
        compiler_params=pltpu.CompilerParams(vmem_limit_bytes=51 * MIB),
    )(pattern, entries)


def arrange_body(kept_ref, *rest):
    *got_refs, near_ref, far_ref = rest
    core, _ = place()

    def put(got_to_ref, kept_to_ref):
        kept_to_ref[...] = kept_ref[...]
        for i, got_ref in enumerate(got_refs):
            size = got_ref.shape[0]
            got_to_ref[i * size : (i + 1) * size, :] = got_ref[...]

    @pl.when(core == 0)
    def _():
        put(far_ref, near_ref)

    @pl.when(core == 1)
    def _():
        put(near_ref, far_ref)


def half(matrix_ref, block_ref, which):
    rows = block_ref.shape[0]
    return dot(matrix_ref[:, which * rows : (which + 1) * rows], block_ref[...])


def window(matrix_ref, first_ref, second_ref):
    return half(matrix_ref, first_ref, 0) + half(matrix_ref, second_ref, 1)


def early_body(own_ref, now_ref, *rest):
    *last, out_ref = rest
    core, _ = place()
    if last:
        far_ref, first_ref, second_ref, before_ref = last
        local = jnp.where(core == 0, now_ref[...], before_ref[...])
        out_ref[...] = dot(own_ref[...], local) + window(far_ref, first_ref, second_ref)
    else:
        local = jnp.where(core == 0, now_ref[...], jnp.zeros_like(now_ref))
        out_ref[...] = dot(own_ref[...], local)


def came(step, pairs, field_ref, history):
    core, pair = place()
    value = jnp.where(pair == pairs - 1, 0.0, field_ref[...].astype(F32))
    if history:
        mine_ref, other_ref = history
        past = jnp.where(pair == step, other_ref[...], mine_ref[...])
        special = jnp.logical_or(pair == step, pair == step + 1)
        value = jnp.where(special, jnp.where(core == 0, past, 0.0), value)
    return value


def add_half(matrix_ref, block_ref, which, early_ref, put):
    rows = block_ref.shape[0]
    size = rows // CHUNKS
    block = block_ref[...]
    columns = slice(which * rows, (which + 1) * rows)
    for i in range(CHUNKS):
        part = slice(i * size, (i + 1) * size)
        put(part, early_ref[part, :] + dot(matrix_ref[part, columns], block))


def first_body(near_ref, first_ref, early_ref, out_ref):
    def put(part, total):
        out_ref[part, :] = total

    add_half(near_ref, first_ref, 0, early_ref, put)


def late_body(step, pairs, near_ref, second_ref, early_ref, field_ref, *rest):
    *history, out_ref = rest
    value = came(step, pairs, field_ref, history)

    def put(part, total):
        out_ref[part, :] = (total + value[part]).astype(BF16)

    add_half(near_ref, second_ref, 1, early_ref, put)


def even_body(step, pairs, near_ref, second_ref, early_ref, *rest):
    total = early_ref[...] + half(near_ref, second_ref, 1)
    if len(rest) == 1:
        rest[0][...] = total
        return
    field_ref, *history, even_ref, out_ref = rest
    total += came(step, pairs, field_ref, history)
    even_ref[...] = total
    out_ref[...] = total.astype(BF16)


def odd_early_body(own_ref, now_ref, out_ref):
    core, _ = place()
    out_ref[...] = dot(own_ref[...], jnp.where(core == 1, now_ref[...], jnp.zeros_like(now_ref)))


def odd_body(which, far_ref, block_ref, early_ref, out_ref):
    out_ref[...] = early_ref[...] + half(far_ref, block_ref, which)


def both_body(which, near_ref, far_ref, block_ref, even_in_ref, odd_in_ref, even_ref, odd_ref):
    even_ref[...] = even_in_ref[...] + half(near_ref, block_ref, which)
    odd_ref[...] = odd_in_ref[...] + half(far_ref, block_ref, which)


def share_body(step, steps, even_ref, odd_ref, *rest):
    *field, keep_ref, send_ref = rest
    core, pair = place()
    even, odd = even_ref[...], odd_ref[...]
    if field:
        ended = pair == step - steps
        came_late = field[0][...].astype(F32)
        even, odd = jnp.where(ended, came_late, even), jnp.where(ended, came_late, odd)
    keep_ref[...] = jnp.where(core == 1, odd, even)
    send_ref[...] = jnp.where(core == 0, odd, even).astype(BF16)


def finish_body(step, steps, mine_ref, other_ref, *rest):
    *earlier, result_ref = rest
    core, pair = place()
    field = mine_ref[...] + other_ref[...].astype(F32)
    if earlier:
        before = earlier[0][...]
        adds = jnp.logical_and(core == 1, pair == step - steps)
        field = jnp.where(
            adds, before + field, jnp.where(pair == step - (steps - 1), field, before)
        )
    result_ref[...] = field


def collect_body(pairs, *refs):
    *seen, out_ref, token_ref = refs
    token_ref[...] = jnp.zeros_like(token_ref)
    _, pair = place()
    for step in range(out_ref.shape[0]):
        value = seen[step][...]
        for later in range(1, pairs):
            value = jnp.where(pair == later, seen[step + later][...], value)
        out_ref[step] = value


def solve(inverse_ref, rhs, out_ref, keep, other):
    size = inverse_ref.shape[1]
    fresh = []
    for i in range(inverse_ref.shape[0]):
        rows = slice(i * size, (i + 1) * size)
        block = dot(inverse_ref[i], rhs[rows]).astype(BF16)
        fresh.append(jnp.where(keep, block, other[rows]))
        out_ref[rows, :] = fresh[-1]
    return fresh


def first_history_body(history_ref, other_history_ref, out_ref):
    core, _ = place()
    out_ref[...] = jnp.where(core == 0, history_ref[...], other_history_ref[...])


def start_body(inverse_ref, excitation_ref, history_ref, out_ref):
    _, pair = place()
    rhs = (excitation_ref[0].astype(F32) - history_ref[...]).astype(BF16)
    solve(inverse_ref, rhs, out_ref, pair == 0, jnp.zeros_like(rhs))


def next_body(step, inverse_ref, excitation_ref, mine_ref, other_ref, came_ref, out_ref, going_ref):
    _, pair = place()
    field = mine_ref[...].astype(F32) + other_ref[...].astype(F32)
    rhs = (excitation_ref[step + 1].astype(F32) - field).astype(BF16)
    first_pair = pair == 0
    size = inverse_ref.shape[1]
    for i, block in enumerate(solve(inverse_ref, rhs, out_ref, first_pair, came_ref)):
        rows = slice(i * size, (i + 1) * size)
        going_ref[rows, :] = jnp.where(first_pair, block, mine_ref[rows, :])


def per_device(lagged_block_entries, pattern, diagonal_block_inverses, excitation, history):
    lags, groups = lax.axis_size("delay"), lax.axis_size("surface")
    pairs = lags // 2
    entries = lagged_block_entries[0]
    blocks, slots, size, _ = entries.shape
    steps, rows, columns = excitation.shape

    def device(d, s):
        return d * groups + s

    def everyone(move):
        return [
            (device(d, s), device(*move(d, s))) for d in range(lags) for s in range(groups)
        ]

    def swapped(value):
        return lax.ppermute(value, AXES, everyone(lambda d, s: (d ^ 1, s)))

    def pair_moved(value, hop):
        return lax.ppermute(value, AXES, everyone(lambda d, s: ((d + 2 * hop) % lags, s)))

    def halo(value, hop, since=0, until=pairs):
        def move(d, s):
            if not since <= d // 2 <= until:
                return d ^ 1, s
            return d, (s + (hop if d % 2 == 0 else -hop)) % groups

        return lax.ppermute(value, AXES, everyone(move))

    other_history = swapped(history[0])
    field_shape = jax.ShapeDtypeStruct((rows, columns), F32)
    current_shape = jax.ShapeDtypeStruct((rows, columns), BF16)
    kept, own, *sent = spread(entries, pattern[0], groups)
    (first_history,) = call(first_history_body, [field_shape], [history[0], other_history])
    (current,) = call(
        start_body,
        [current_shape],
        [diagonal_block_inverses, excitation, first_history],
    )
    matrix_shape = jax.ShapeDtypeStruct((rows, 2 * rows), kept.dtype)
    near, far = call(arrange_body, [matrix_shape, matrix_shape], [kept] + [swapped(part) for part in sent])

    going = field = current
    seen = []
    previous = []
    result = None
    out = collected = None
    rounds = steps + pairs - 1
    windows = None
    for step in range(rounds):
        seen.append(current)
        if step == rounds - 1:
            out, collected = call(
                functools.partial(collect_body, pairs),
                [jax.ShapeDtypeStruct(excitation.shape, BF16), TOKEN],
                seen,
            )
        first, second = windows or (halo(current, 1, 0, step), halo(current, 2, 0, step))
        if pairs == 2:
            current_in = field_in = pair_moved(going, 1)
        else:
            current_in, field_in = pair_moved(current, 1), pair_moved(field, -1)
        last = [far, *previous] if previous else []
        ending = max(step - (steps - 1), 0)
        going_on = functools.partial(only, ending, pairs)
        (early,) = call(
            functools.partial(going_on, 1, early_body), [field_shape], [own, current] + last
        )
        (partly,) = call(
            functools.partial(going_on, 1, first_body), [field_shape], [near, first, early]
        )
        received = [near, second, partly]
        past = [history[0], other_history] if step < pairs else []
        previous = [first, second, current]
        if step < steps - 1:
            (field,) = call(
                functools.partial(late_body, step, pairs),
                [current_shape],
                received + [field_in] + past,
                in_front=len(received) if step == 1 else None,
            )
            current, going = call(
                functools.partial(next_body, step),
                [current_shape, current_shape],
                [diagonal_block_inverses, excitation, field, swapped(field), current_in],
            )
        else:
            if step < rounds - 1:
                done = step + 2 - steps
                windows = halo(current_in, 1, done), halo(current_in, 2, done)
            more = step < rounds - 1
            alone = functools.partial(only, ending, ending, 1)
            (odd_early,) = call(
                functools.partial(alone, odd_early_body), [field_shape], [own, current]
            )
            if more:
                even, *next_field = call(
                    functools.partial(going_on, 1 + more, functools.partial(even_body, step, pairs)),
                    [field_shape] + [current_shape] * more,
                    received + ([field_in] + past) * more,
                )
                for which, block in enumerate((first, second)):
                    (odd_early,) = call(
                        functools.partial(alone, functools.partial(odd_body, which)),
                        [field_shape],
                        [far, block, odd_early],
                    )
            else:
                even, next_field = early, []
                for which, block in enumerate((first, second)):
                    even, odd_early = call(
                        functools.partial(
                            only, ending, ending, 2, functools.partial(both_body, which)
                        ),
                        [field_shape, field_shape],
                        [near, far, block, even, odd_early],
                    )
            mine, send = call(
                functools.partial(share_body, step, steps),
                [field_shape, current_shape],
                [even, odd_early] + [field_in] * (step >= steps),
            )
            (result,) = call(
                functools.partial(finish_body, step, steps),
                [field_shape],
                [mine, swapped(send)] + [result] * (step >= steps),
                after=collected,
            )
            field = next_field[0] if next_field else None
            current, going = current_in, field
    return (out, result[None])


def solution(mesh):
    placed = (
        P("delay", "surface", None, None, None),
        P("delay", "surface", None),
        P("surface", None, None),
        P(None, "surface", None),
        P("delay", "surface", None),
    )
    return jax.shard_map(
        per_device,
        mesh=mesh,
        in_specs=placed,
        out_specs=(P(None, "surface", None), P("delay", "surface", None)),
        check_vma=False,
    )
```

```python
import functools

import jax
import jax.numpy as jnp
from jax import lax
from jax.experimental import pallas as pl
from jax.experimental.pallas import tpu as pltpu
from jax.sharding import PartitionSpec as P

F32 = jnp.float32
BF16 = jnp.bfloat16
AXES = ("delay", "surface")
VMEM = pl.BlockSpec(memory_space=pltpu.VMEM)
MIB = 1024 * 1024
CHUNKS = 2
TOKEN = jax.ShapeDtypeStruct((8, 128), F32)


def dot(a, b):
    return jnp.dot(a, b, preferred_element_type=F32)


def place():
    lag = lax.axis_index("delay")
    return lax.rem(lag, 2), lax.div(lag, 2)


COST = pl.CostEstimate(flops=0, bytes_accessed=1 << 20, transcendentals=0)


def call(body, outs, args, after=None, in_front=None):
    specs = [VMEM] * len(args)
    if in_front is not None:
        args = args[in_front : in_front + 1] + args[:in_front] + args[in_front + 1 :]
        body = functools.partial(put_back, body, in_front)
    if after is not None:
        body = functools.partial(skip, body, len(args))
        args, specs = args + [after], specs + [pl.BlockSpec(memory_space=pl.ANY)]
    return pl.pallas_call(
        body,
        out_shape=tuple(outs),
        in_specs=specs,
        out_specs=tuple(VMEM for _ in outs),
        cost_estimate=COST,
        compiler_params=pltpu.CompilerParams(vmem_limit_bytes=8 * MIB),
    )(*args)


def only(lowest, highest, outs, body, *refs):
    _, pair = place()
    wanted = jnp.logical_and(pair >= lowest, pair <= highest)

    @pl.when(wanted)
    def _():
        body(*refs)

    @pl.when(jnp.logical_not(wanted))
    def _():
        for ref in refs[len(refs) - outs :]:
            ref[...] = jnp.zeros_like(ref)


def put_back(body, in_front, moved, *refs):
    body(*refs[:in_front], moved, *refs[in_front:])


def skip(body, number, *refs):
    body(*refs[:number], *refs[number + 1 :])


def spread_body(groups, pattern_ref, entries_ref, keep_ref, own_ref, *rest):
    *send_refs, here_ref, all_ref, slots_ref, sems, slots_sem = rest
    core, _ = place()
    blocks, slots, size, _ = entries_ref.shape
    slots_copy = pltpu.make_async_copy(pattern_ref, slots_ref, slots_sem)
    slots_copy.start()
    copies = [
        pltpu.make_async_copy(entries_ref.at[row], here_ref.at[row], sems.at[row])
        for row in range(blocks)
    ]
    for copy in copies:
        copy.start()
    base = (lax.axis_index("surface") - 2) * blocks
    total = groups * blocks
    all_ref[...] = jnp.zeros_like(all_ref)
    slots_copy.wait()
    width = 2 * blocks * size
    mine = pl.ds(pl.multiple_of(core * width, width), width)
    other = pl.ds(pl.multiple_of((1 - core) * width, width), width)
    for row in range(blocks):
        copies[row].wait()
        rows = slice(row * size, (row + 1) * size)
        for slot in range(slots):
            j = lax.rem(slots_ref[row, slot] - base + total, total)
            column = jnp.where(
                j < 2 * blocks,
                jnp.where(j < blocks, j + blocks, j - blocks),
                jnp.where(j < 3 * blocks, j + 2 * blocks, j - blocks),
            )
            columns = pl.ds(pl.multiple_of(column * size, size), size)
            all_ref[rows, columns] = here_ref[row, slot]
        keep_ref[rows, :] = all_ref[rows, mine]
        own_ref[rows, :] = all_ref[rows, 2 * width :]
        send_refs[row][...] = all_ref[rows, other]


def spread(entries, pattern, groups):
    blocks, slots, size, _ = entries.shape
    side = blocks * size

    def matrix(rows, columns):
        return jax.ShapeDtypeStruct((rows, columns), entries.dtype)

    return pl.pallas_call(
        functools.partial(spread_body, groups),
        out_shape=(matrix(side, 2 * side), matrix(side, side), *[matrix(size, 2 * side)] * blocks),
        in_specs=[pl.BlockSpec(memory_space=pl.ANY)] * 2,
        out_specs=(VMEM,) * (blocks + 2),
        scratch_shapes=[
            pltpu.VMEM(entries.shape, entries.dtype),
            pltpu.VMEM((side, 5 * side), entries.dtype),
            pltpu.SMEM(pattern.shape, pattern.dtype),
            pltpu.SemaphoreType.DMA((blocks,)),
            pltpu.SemaphoreType.DMA,
        ],
        cost_estimate=COST,
        compiler_params=pltpu.CompilerParams(vmem_limit_bytes=51 * MIB),
    )(pattern, entries)


def arrange_body(kept_ref, *rest):
    *got_refs, near_ref, far_ref = rest
    core, _ = place()

    def put(got_to_ref, kept_to_ref):
        kept_to_ref[...] = kept_ref[...]
        for i, got_ref in enumerate(got_refs):
            size = got_ref.shape[0]
            got_to_ref[i * size : (i + 1) * size, :] = got_ref[...]

    @pl.when(core == 0)
    def _():
        put(far_ref, near_ref)

    @pl.when(core == 1)
    def _():
        put(near_ref, far_ref)


def half(matrix_ref, block_ref, which):
    rows = block_ref.shape[0]
    return dot(matrix_ref[:, which * rows : (which + 1) * rows], block_ref[...])


def window(matrix_ref, first_ref, second_ref):
    return half(matrix_ref, first_ref, 0) + half(matrix_ref, second_ref, 1)


def early_body(own_ref, now_ref, *rest):
    *last, out_ref = rest
    core, _ = place()
    if last:
        far_ref, first_ref, second_ref, before_ref = last
        local = jnp.where(core == 0, now_ref[...], before_ref[...])
        out_ref[...] = dot(own_ref[...], local) + window(far_ref, first_ref, second_ref)
    else:
        local = jnp.where(core == 0, now_ref[...], jnp.zeros_like(now_ref))
        out_ref[...] = dot(own_ref[...], local)


def came(step, pairs, field_ref, history):
    core, pair = place()
    value = jnp.where(pair == pairs - 1, 0.0, field_ref[...].astype(F32))
    if history:
        mine_ref, other_ref = history
        past = jnp.where(pair == step, other_ref[...], mine_ref[...])
        special = jnp.logical_or(pair == step, pair == step + 1)
        value = jnp.where(special, jnp.where(core == 0, past, 0.0), value)
    return value


def add_half(matrix_ref, block_ref, which, early_ref, put):
    rows = block_ref.shape[0]
    size = rows // CHUNKS
    block = block_ref[...]
    columns = slice(which * rows, (which + 1) * rows)
    for i in range(CHUNKS):
        part = slice(i * size, (i + 1) * size)
        put(part, early_ref[part, :] + dot(matrix_ref[part, columns], block))


def first_body(near_ref, first_ref, early_ref, out_ref):
    def put(part, total):
        out_ref[part, :] = total

    add_half(near_ref, first_ref, 0, early_ref, put)


def late_body(step, pairs, near_ref, second_ref, early_ref, field_ref, *rest):
    *history, out_ref = rest
    value = came(step, pairs, field_ref, history)

    def put(part, total):
        out_ref[part, :] = (total + value[part]).astype(BF16)

    add_half(near_ref, second_ref, 1, early_ref, put)


def even_body(step, pairs, near_ref, second_ref, early_ref, *rest):
    total = early_ref[...] + half(near_ref, second_ref, 1)
    if len(rest) == 1:
        rest[0][...] = total
        return
    field_ref, *history, even_ref, out_ref = rest
    total += came(step, pairs, field_ref, history)
    even_ref[...] = total
    out_ref[...] = total.astype(BF16)


def odd_early_body(own_ref, now_ref, out_ref):
    core, _ = place()
    out_ref[...] = dot(own_ref[...], jnp.where(core == 1, now_ref[...], jnp.zeros_like(now_ref)))


def odd_body(which, far_ref, block_ref, early_ref, out_ref):
    out_ref[...] = early_ref[...] + half(far_ref, block_ref, which)


def share_body(step, steps, even_ref, odd_ref, *rest):
    *field, keep_ref, send_ref = rest
    core, pair = place()
    even, odd = even_ref[...], odd_ref[...]
    if field:
        ended = pair == step - steps
        came_late = field[0][...].astype(F32)
        even, odd = jnp.where(ended, came_late, even), jnp.where(ended, came_late, odd)
    keep_ref[...] = jnp.where(core == 1, odd, even)
    send_ref[...] = jnp.where(core == 0, odd, even).astype(BF16)


def finish_body(step, steps, mine_ref, other_ref, *rest):
    *earlier, result_ref = rest
    core, pair = place()
    field = mine_ref[...] + other_ref[...].astype(F32)
    if earlier:
        before = earlier[0][...]
        adds = jnp.logical_and(core == 1, pair == step - steps)
        field = jnp.where(
            adds, before + field, jnp.where(pair == step - (steps - 1), field, before)
        )
    result_ref[...] = field


def collect_body(pairs, *refs):
    *seen, out_ref, token_ref = refs
    token_ref[...] = jnp.zeros_like(token_ref)
    _, pair = place()
    for step in range(out_ref.shape[0]):
        value = seen[step][...]
        for later in range(1, pairs):
            value = jnp.where(pair == later, seen[step + later][...], value)
        out_ref[step] = value


def solve(inverse_ref, rhs, out_ref, keep, other):
    size = inverse_ref.shape[1]
    fresh = []
    for i in range(inverse_ref.shape[0]):
        rows = slice(i * size, (i + 1) * size)
        block = dot(inverse_ref[i], rhs[rows]).astype(BF16)
        fresh.append(jnp.where(keep, block, other[rows]))
        out_ref[rows, :] = fresh[-1]
    return fresh


def start_body(inverse_ref, excitation_ref, history_ref, other_history_ref, out_ref):
    core, pair = place()
    history = jnp.where(core == 0, history_ref[...], other_history_ref[...])
    rhs = (excitation_ref[0].astype(F32) - history).astype(BF16)
    solve(inverse_ref, rhs, out_ref, pair == 0, jnp.zeros_like(rhs))


def next_body(step, inverse_ref, excitation_ref, mine_ref, other_ref, came_ref, out_ref, going_ref):
    _, pair = place()
    field = mine_ref[...].astype(F32) + other_ref[...].astype(F32)
    rhs = (excitation_ref[step + 1].astype(F32) - field).astype(BF16)
    first_pair = pair == 0
    size = inverse_ref.shape[1]
    for i, block in enumerate(solve(inverse_ref, rhs, out_ref, first_pair, came_ref)):
        rows = slice(i * size, (i + 1) * size)
        going_ref[rows, :] = jnp.where(first_pair, block, mine_ref[rows, :])


def per_device(lagged_block_entries, pattern, diagonal_block_inverses, excitation, history):
    lags, groups = lax.axis_size("delay"), lax.axis_size("surface")
    pairs = lags // 2
    entries = lagged_block_entries[0]
    blocks, slots, size, _ = entries.shape
    steps, rows, columns = excitation.shape

    def device(d, s):
        return d * groups + s

    def everyone(move):
        return [
            (device(d, s), device(*move(d, s))) for d in range(lags) for s in range(groups)
        ]

    def swapped(value):
        return lax.ppermute(value, AXES, everyone(lambda d, s: (d ^ 1, s)))

    def pair_moved(value, hop):
        return lax.ppermute(value, AXES, everyone(lambda d, s: ((d + 2 * hop) % lags, s)))

    def halo(value, hop, since=0, until=pairs):
        def move(d, s):
            if not since <= d // 2 <= until:
                return d ^ 1, s
            return d, (s + (hop if d % 2 == 0 else -hop)) % groups

        return lax.ppermute(value, AXES, everyone(move))

    other_history = swapped(history[0])
    field_shape = jax.ShapeDtypeStruct((rows, columns), F32)
    current_shape = jax.ShapeDtypeStruct((rows, columns), BF16)
    kept, own, *sent = spread(entries, pattern[0], groups)
    (current,) = call(
        start_body,
        [current_shape],
        [diagonal_block_inverses, excitation, history[0], other_history],
    )
    matrix_shape = jax.ShapeDtypeStruct((rows, 2 * rows), kept.dtype)
    near, far = call(arrange_body, [matrix_shape, matrix_shape], [kept] + [swapped(part) for part in sent])

    going = field = current
    seen = []
    previous = []
    result = None
    out = collected = None
    rounds = steps + pairs - 1
    windows = None
    for step in range(rounds):
        seen.append(current)
        if step == rounds - 1:
            out, collected = call(
                functools.partial(collect_body, pairs),
                [jax.ShapeDtypeStruct(excitation.shape, BF16), TOKEN],
                seen,
            )
        first, second = windows or (halo(current, 1, 0, step), halo(current, 2, 0, step))
        if pairs == 2:
            current_in = field_in = pair_moved(going, 1)
        else:
            current_in, field_in = pair_moved(current, 1), pair_moved(field, -1)
        last = [far, *previous] if previous else []
        ending = max(step - (steps - 1), 0)
        going_on = functools.partial(only, ending, pairs)
        (early,) = call(
            functools.partial(going_on, 1, early_body), [field_shape], [own, current] + last
        )
        (partly,) = call(
            functools.partial(going_on, 1, first_body), [field_shape], [near, first, early]
        )
        received = [near, second, partly]
        past = [history[0], other_history] if step < pairs else []
        previous = [first, second, current]
        if step < steps - 1:
            (field,) = call(
                functools.partial(late_body, step, pairs),
                [current_shape],
                received + [field_in] + past,
                in_front=len(received) if step == 1 else None,
            )
            current, going = call(
                functools.partial(next_body, step),
                [current_shape, current_shape],
                [diagonal_block_inverses, excitation, field, swapped(field), current_in],
            )
        else:
            if step < rounds - 1:
                done = step + 2 - steps
                windows = halo(current_in, 1, done), halo(current_in, 2, done)
            more = step < rounds - 1
            even, *next_field = call(
                functools.partial(going_on, 1 + more, functools.partial(even_body, step, pairs)),
                [field_shape] + [current_shape] * more,
                received + ([field_in] + past) * more,
            )
            alone = functools.partial(only, ending, ending, 1)
            (odd_early,) = call(
                functools.partial(alone, odd_early_body), [field_shape], [own, current]
            )
            for which, block in enumerate((first, second)):
                (odd_early,) = call(
                    functools.partial(alone, functools.partial(odd_body, which)),
                    [field_shape],
                    [far, block, odd_early],
                )
            mine, send = call(
                functools.partial(share_body, step, steps),
                [field_shape, current_shape],
                [even, odd_early] + [field_in] * (step >= steps),
            )
            (result,) = call(
                functools.partial(finish_body, step, steps),
                [field_shape],
                [mine, swapped(send)] + [result] * (step >= steps),
                after=collected,
            )
            field = next_field[0] if more else None
            current, going = current_in, field
    return (out, result[None])


def solution(mesh):
    placed = (
        P("delay", "surface", None, None, None),
        P("delay", "surface", None),
        P("surface", None, None),
        P(None, "surface", None),
        P("delay", "surface", None),
    )
    return jax.shard_map(
        per_device,
        mesh=mesh,
        in_specs=placed,
        out_specs=(P(None, "surface", None), P("delay", "surface", None)),
        check_vma=False,
    )
```
